32 devices in a mesh: freq: 8 (over z, core), tm: 2 (over y), beam: 2 (over x).
Axes of the slice: x: 2, y: 2, z: 4, core: 2. Of those that a mesh axis runs over, the one named last changes fastest.
Arguments:
- raw_samples: bfloat16 [6144, 4096], P(('beam', 'tm'), 'freq'), parts along dimension 0, may hold values from -6 to 6
- filter_taps: bfloat16 [16, 4096], P(None, 'freq'), may hold values from -1.5 to 1.5
- dm_trials: int32 [256], replicated, may hold values from 0 to 1024, as said below
- channel_units: int32 [4096], replicated, may hold values from 0 to 512, as said below
Outputs:
- dm_power: float32 [4, 256, 256], P(('beam', 'tm'), 'freq'), parts along dimension 0
The draws below stay inside these ranges and needn't reach their ends.
There are 2 independent parts, one for each index of `beam`. The reference program is written for one: setup_inputs(seed, part) draws one part's arguments, and reference() takes and returns one part's arrays. A program takes and returns all parts, laid end to end along the dimension named above; an argument that names none is the same for every part. Nothing has to cross between parts.
Inputs may be any that keep to these rules, and one draw needn't show every extreme that they name: Trial d delays a channel of integer delay u by floor(dm_trials[d] * u / 1024) frames. `channel_units`: so that no dispersion delay exceeds 512 frames.
All inputs are finite; a program needn't handle non-finite values.
Results may differ from the reference program's by a relative error of at most 0.0072.
Values may be sent and summed in bfloat16 or wider, within the bound.
A program may use at most 64 MiB of HBM per device.

```python
import math
import jax
import jax.numpy as jnp
from jax import lax

CHANNELS = 4096
TAPS = 16
DFT_LEN = 2048
BINS = 256
SHARED = 512
DMS = 256
DM_STEPS = 1024
SEGS_DEV = 1
SEGMENTS = 2
FRAMES = 3072
N_FREQ = 8
N_TM = 2


def draw_dm_trials(key, part):
    values = jax.random.randint(jax.random.fold_in(key, 11), (DMS,), 0, DM_STEPS + 1, dtype=jnp.int32)
    marked = jax.random.randint(jax.random.fold_in(key, 12), (), 0, DMS, dtype=jnp.int32)
    return jnp.where(jnp.arange(DMS, dtype=jnp.int32) == marked, DM_STEPS, values).astype(jnp.int32)


def draw_channel_units(key, part):
    values = jax.random.randint(jax.random.fold_in(key, 21), (CHANNELS,), 0, SHARED + 1, dtype=jnp.int32)
    marked = jax.random.randint(jax.random.fold_in(key, 22), (), 0, CHANNELS, dtype=jnp.int32)
    return jnp.where(jnp.arange(CHANNELS, dtype=jnp.int32) == marked, SHARED, values).astype(jnp.int32)


def block_levels(own_key, shape, shards, smallest, largest):
    gain, own = 1.0, jax.random.fold_in(own_key, 6)
    for axis_at, blocks in shards:
        draws = jnp.exp(jax.random.uniform(jax.random.fold_in(own, axis_at), (blocks,), jnp.float32, smallest / len(shards), largest / len(shards)))
        gain = gain * jnp.repeat(draws, shape[axis_at] // blocks).reshape([-1 if axis == axis_at else 1 for axis in range(len(shape))])
    return gain


def centred(rng, shape, scale, limit, split=(), kind=jnp.bfloat16):
    gain = block_levels(rng, shape, split, -0.22, 0.18) if split else 1.0
    array = jax.random.normal(rng, shape, jnp.float32) * scale * gain
    return jnp.minimum(jnp.maximum(array, -limit), limit).astype(kind)


def setup_inputs(seed: int = 0, part: int = 0) -> dict:
    seeds = jax.random.split(jax.random.key(seed), 5)
    part_splits = jax.random.split(jax.random.fold_in(seeds[4], part), 5)
    raw_samples = centred(part_splits[0], (FRAMES, CHANNELS), 1.0, 6.0, ((0, 2), (1, 8)))
    filter_taps = centred(seeds[1], (TAPS, CHANNELS), TAPS ** -0.5, 1.5, ((1, 8),))
    dm_trials = draw_dm_trials(jax.random.fold_in(seeds[4], 71), part)
    channel_units = draw_channel_units(jax.random.fold_in(seeds[4], 71), part)
    return dict(raw_samples=raw_samples, filter_taps=filter_taps, dm_trials=dm_trials, channel_units=channel_units)


ramp_block = 32

def rounded(values):
    return lax.optimization_barrier(values.astype(jnp.bfloat16)).astype(jnp.float32)

def reference(raw_samples, filter_taps, dm_trials, channel_units):
    members = N_FREQ
    inner_len = CHANNELS // members
    step_len = DFT_LEN - SHARED
    own_len = SEGS_DEV * step_len
    frames = own_len + SHARED
    highest = lax.Precision.HIGHEST
    padded = jnp.pad(raw_samples.astype(jnp.float32), ((TAPS - 1, SHARED), (0, 0)))
    taps_wide = filter_taps.astype(jnp.float32)
    source = jnp.arange(members, dtype=jnp.int32)
    inner_ids = jnp.arange(inner_len, dtype=jnp.int32)
    phases_one = (inner_len * source[:, None, None] * source[None, None, :] + inner_ids[None, :, None] * source[None, None, :]) % CHANNELS
    angles_one = phases_one.astype(jnp.float32) * (2.0 * math.pi / CHANNELS)
    scale_one = 1.0 / math.sqrt(members)
    cos_one = rounded(jnp.cos(angles_one) * scale_one)
    sin_one = rounded(jnp.sin(angles_one) * scale_one)
    phases_two = inner_ids[:, None] * inner_ids[None, :] % inner_len
    angles_two = phases_two.astype(jnp.float32) * (2.0 * math.pi / inner_len)
    scale_two = 1.0 / math.sqrt(inner_len)
    cos_two = rounded(jnp.cos(angles_two) * scale_two)
    sin_two = rounded(jnp.sin(angles_two) * scale_two)
    bin_all = jnp.arange(BINS, dtype=jnp.int32)
    time_ids = jnp.arange(DFT_LEN, dtype=jnp.int32)
    phases_three = bin_all[:, None] * time_ids[None, :] % DFT_LEN
    angles_three = phases_three.astype(jnp.float32) * (2.0 * math.pi / DFT_LEN)
    scale_three = 1.0 / math.sqrt(DFT_LEN)
    cos_three = rounded(jnp.cos(angles_three) * scale_three)
    sin_three = rounded(jnp.sin(angles_three) * scale_three)

    def channelize(block_id):
        extended = lax.dynamic_slice_in_dim(padded, block_id * own_len, frames + TAPS - 1, 0)
        total = jnp.zeros((frames, CHANNELS), jnp.float32)
        for tap_id in range(TAPS):
            total = total + taps_wide[tap_id] * extended[TAPS - 1 - tap_id:TAPS - 1 - tap_id + frames]
        filtered = rounded(total)
        seg_reals = []
        seg_imags = []
        for seg_id in range(SEGS_DEV):
            piece = filtered[seg_id * step_len:seg_id * step_len + DFT_LEN]
            seg_reals.append(jnp.dot(cos_three, piece, precision=highest))
            seg_imags.append(-jnp.dot(sin_three, piece, precision=highest))
        seg_real = jnp.stack(seg_reals).reshape(SEGS_DEV * BINS, members, inner_len)
        seg_imag = jnp.stack(seg_imags).reshape(SEGS_DEV * BINS, members, inner_len)
        first_real = jnp.einsum('tfa,fak->tak', seg_real, cos_one, precision=highest) + jnp.einsum('tfa,fak->tak', seg_imag, sin_one, precision=highest)
        first_imag = jnp.einsum('tfa,fak->tak', seg_imag, cos_one, precision=highest) - jnp.einsum('tfa,fak->tak', seg_real, sin_one, precision=highest)
        chan_real = jnp.einsum('tak,am->tmk', first_real, cos_two, precision=highest) + jnp.einsum('tak,am->tmk', first_imag, sin_two, precision=highest)
        chan_imag = jnp.einsum('tak,am->tmk', first_imag, cos_two, precision=highest) - jnp.einsum('tak,am->tmk', first_real, sin_two, precision=highest)
        chan_real = rounded(chan_real).reshape(SEGS_DEV, BINS, CHANNELS)
        chan_imag = rounded(chan_imag).reshape(SEGS_DEV, BINS, CHANNELS)
        return jnp.stack([chan_real, chan_imag], axis=1)
    spectra = lax.map(channelize, jnp.arange(N_TM, dtype=jnp.int32))
    spectra = jnp.transpose(spectra, (3, 4, 0, 1, 2)).reshape(BINS, CHANNELS, SEGMENTS * 2)
    delays = dm_trials[:, None] * channel_units[None, :] // DM_STEPS
    norm = 1.0 / math.sqrt(CHANNELS)

    def ramp_piece(block_id):
        bin_ids = block_id * ramp_block + jnp.arange(ramp_block, dtype=jnp.int32)
        phases = bin_ids[:, None, None] * delays[None, :, :] % DFT_LEN
        angles = phases.astype(jnp.float32) * (2.0 * math.pi / DFT_LEN)
        cosine = rounded(jnp.cos(angles))
        sine = rounded(jnp.sin(angles))
        piece = lax.dynamic_slice_in_dim(spectra, block_id * ramp_block, ramp_block, 0)
        cos_part = jnp.einsum('bdc,bcx->bdx', cosine, piece, precision=highest)
        sin_part = jnp.einsum('bdc,bcx->bdx', sine, piece, precision=highest)
        return (cos_part, sin_part)
    cos_part, sin_part = lax.map(ramp_piece, jnp.arange(BINS // ramp_block, dtype=jnp.int32))
    cos_part = cos_part.reshape(BINS, DMS, SEGMENTS, 2)
    sin_part = sin_part.reshape(BINS, DMS, SEGMENTS, 2)
    real_part = (cos_part[..., 0] - sin_part[..., 1]) * norm
    imag_part = (sin_part[..., 0] + cos_part[..., 1]) * norm
    return jnp.transpose(real_part * real_part + imag_part * imag_part, (2, 1, 0))
```

```python
import functools
import math

import jax
import jax.numpy as jnp
import numpy as np
from jax import lax
from jax.experimental import pallas as pl
from jax.experimental.pallas import tpu as pltpu
from jax.sharding import PartitionSpec as P

TAPS = 16
DFT_LEN = 2048
BINS = 256
SHARED = 512
DMS = 256
DM_STEPS = 1024
CHANNELS = 4096
RADIX = 8
INNER = CHANNELS // RADIX
CHUNK = 16
LANES = 128


def tables():
    bins = np.arange(BINS)[:, None]
    angle = 2 * np.pi * (bins * np.arange(DFT_LEN)[None, :] % DFT_LEN) / DFT_LEN
    time = np.concatenate([np.cos(angle), -np.sin(angle)], 0) / math.sqrt(DFT_LEN)
    angle = 2 * np.pi * (bins * np.arange(TAPS)[None, :]) / DFT_LEN
    tap = np.concatenate([np.cos(angle), -np.sin(angle)], 0)
    ids = np.arange(INNER)
    angle = 2 * np.pi * (np.arange(RADIX)[:, None] * ids[None, :]) / CHANNELS
    twiddle = np.stack([np.cos(angle), -np.sin(angle)]) / math.sqrt(RADIX)
    spread = ids.reshape(CHANNELS // LANES, LANES // RADIX).T.reshape(-1)
    angle = 2 * np.pi * (ids[:, None] * spread[None, :] % INNER) / INNER
    cosine, sine = np.cos(angle), np.sin(angle)
    channel = np.block([[cosine, -sine], [sine, cosine]]) / math.sqrt(INNER)
    return (
        jnp.asarray(time, jnp.bfloat16),
        jnp.asarray(tap, jnp.float32),
        jnp.asarray(twiddle, jnp.float32),
        jnp.asarray(channel, jnp.bfloat16),
    )


def unit_circle(phase):
    x = phase.astype(jnp.float32) * (2.0 * math.pi / DFT_LEN)
    y = x * x
    sine, cosine = jnp.full_like(y, -1 / 39916800), jnp.full_like(y, 1 / 479001600)
    for value in (1 / 362880, -1 / 5040, 1 / 120, -1 / 6, 1.0):
        sine = sine * y + value
    for value in (-1 / 3628800, 1 / 40320, -1 / 720, 1 / 24, -0.5, 1.0):
        cosine = cosine * y + value
    return cosine, sine * x


def fill_ramps(ramps, dms, first_bin, start, stop):
    bins = ramps.shape[0]

    @pl.loop(start, stop)
    def _(step):
        row = pl.multiple_of(step * CHUNK, CHUNK)
        units = lax.broadcasted_iota(jnp.int32, (CHUNK, DMS), 0) + (row + 1)
        delays = (units * dms[...]) >> 10
        turn_cos, turn_sin = unit_circle(delays)
        phase = (delays * first_bin) & (DFT_LEN - 1)
        quarter = phase >> 9
        cosine, sine = unit_circle(phase & 511)
        odd = (quarter & 1) == 1
        swapped_cos = jnp.where(odd, -sine, cosine)
        swapped_sin = jnp.where(odd, cosine, sine)
        far = quarter >= 2
        cosine = jnp.where(far, -swapped_cos, swapped_cos)
        sine = jnp.where(far, -swapped_sin, swapped_sin)
        for at in range(bins):
            ramps[at, pl.ds(row, CHUNK), :] = cosine.astype(jnp.bfloat16)
            ramps[at, pl.ds(SHARED + row, CHUNK), :] = sine.astype(jnp.bfloat16)
            if at + 1 < bins:
                cosine, sine = (
                    cosine * turn_cos - sine * turn_sin,
                    sine * turn_cos + cosine * turn_sin,
                )


def dft(real, imag):
    count = len(real)
    if count == 1:
        return real, imag
    er, ei = dft(real[0::2], imag[0::2])
    odr, odi = dft(real[1::2], imag[1::2])
    half = count // 2
    outs = [None] * count
    for k in range(half):
        if k == 0:
            tr, ti = odr[k], odi[k]
        elif 4 * k == count:
            tr, ti = odi[k], -odr[k]
        else:
            c, s = math.cos(2 * math.pi * k / count), math.sin(2 * math.pi * k / count)
            tr, ti = odr[k] * c + odi[k] * s, odi[k] * c - odr[k] * s
        outs[k] = (er[k] + tr, ei[k] + ti)
        outs[k + half] = (er[k] - tr, ei[k] - ti)
    return [o[0] for o in outs], [o[1] for o in outs]


def channelize(held, twiddle, first, slab):
    slabs, members, _, bins, _ = held.shape
    per = members // RADIX
    for src in range(per):
        lane = src * slabs + slab
        real, imag = [], []
        for n2 in range(RADIX):
            real.append(held[slab, n2 * per + src, 0].astype(jnp.float32))
            imag.append(held[slab, n2 * per + src, 1].astype(jnp.float32))
        real, imag = dft(real, imag)
        cols = slice(lane * 128, lane * 128 + 128)
        cols_imag = slice(INNER + lane * 128, INNER + lane * 128 + 128)
        for k2 in range(RADIX):
            c, s = twiddle[0, k2 : k2 + 1, cols], twiddle[1, k2 : k2 + 1, cols]
            rows = slice(k2 * bins, k2 * bins + bins)
            first[rows, cols] = real[k2] * c - imag[k2] * s
            first[rows, cols_imag] = real[k2] * s + imag[k2] * c


def fill_matches(matches, units):
    rows, lanes = units.shape
    ids = lax.broadcasted_iota(jnp.int32, (rows, SHARED), 1) + 1
    for k2 in range(RADIX):
        for at in range(lanes // RADIX):
            lane = at * RADIX + k2
            same = (units[:, lane : lane + 1] == ids).astype(jnp.float32)
            matches[k2, at * rows : (at + 1) * rows, :] = same.astype(jnp.bfloat16)


def group_units(spectra, matches, bins):
    grouped = jnp.zeros((2 * bins, SHARED), jnp.float32)
    whole = jnp.zeros((2 * bins, INNER), jnp.float32)
    for k2 in range(RADIX):
        part = spectra[k2 * bins : (k2 + 1) * bins]
        part = jnp.concatenate([part[:, :INNER], part[:, INNER:]], 0)
        part = part.astype(jnp.bfloat16)
        whole += part.astype(jnp.float32)
        grouped += jnp.dot(part, matches[k2], preferred_element_type=jnp.float32)
    rest = jnp.sum(whole, 1, keepdims=True) - jnp.sum(grouped, 1, keepdims=True)
    return grouped, rest


def partner_order(members):
    return sorted(range(1, members), key=lambda o: -abs(o - members // 2))


def kernel(
    members, segments,
    raw, time_hbm, channel_hbm, filter_taps, units, dms, tap, twiddle,
    out,
    own, time, channel, later, tail, padded, spec, gain, extra, outgoing, held,
    ramps, matches, first, power_out, power_in,
    local_sem, halo_send, halo_recv, seg_send, seg_recv, pow_send, pow_recv,
):
    me = lax.axis_index("freq")
    seg = lax.axis_index("tm")
    own_len, width = own.shape
    bins = BINS // members
    kept = DMS // members
    loads = [
        pltpu.make_async_copy(raw, own, local_sem.at[0]),
        pltpu.make_async_copy(time_hbm, time, local_sem.at[1]),
        pltpu.make_async_copy(channel_hbm, channel, local_sem.at[2]),
    ]
    for load in loads[:2]:
        load.start()

    barrier = pltpu.get_barrier_semaphore()
    order = partner_order(members)
    for o in order:
        pl.semaphore_signal(
            barrier, inc=1, device_id={"freq": lax.rem(me + o, members)},
            device_id_type=pl.DeviceIdType.MESH,
        )

    @pl.when(seg > 0)
    def _():
        pl.semaphore_signal(
            barrier, inc=1, device_id={"tm": seg - 1}, device_id_type=pl.DeviceIdType.MESH
        )

    @pl.when(seg < segments - 1)
    def _():
        pl.semaphore_signal(
            barrier, inc=1, device_id={"tm": seg + 1}, device_id_type=pl.DeviceIdType.MESH
        )

    pl.semaphore_wait(
        barrier, members - 1 + jnp.minimum(seg, 1) + jnp.minimum(segments - 1 - seg, 1)
    )

    slabs = width // LANES

    def back_copy(slab):
        return pltpu.make_async_remote_copy(
            src_ref=raw.at[pl.ds(0, SHARED), pl.ds(slab * LANES, LANES)],
            dst_ref=later.at[slab],
            send_sem=halo_send.at[1 + slab], recv_sem=halo_recv.at[1 + slab],
            device_id={"tm": seg - 1}, device_id_type=pl.DeviceIdType.MESH,
        )

    def forward_copy():
        return pltpu.make_async_remote_copy(
            src_ref=raw.at[pl.ds(own_len - TAPS, TAPS)], dst_ref=tail,
            send_sem=halo_send.at[0], recv_sem=halo_recv.at[0],
            device_id={"tm": seg + 1}, device_id_type=pl.DeviceIdType.MESH,
        )

    @pl.when(seg > 0)
    def _():
        for slab in range(slabs):
            back_copy(slab).start()

    @pl.when(seg == 0)
    def _():
        tail[...] = jnp.zeros_like(tail)

    @pl.when(seg < segments - 1)
    def _():
        forward_copy().start()

    @pl.when(seg == segments - 1)
    def _():
        later[...] = jnp.zeros_like(later)

    loads[2].start()
    taps = filter_taps[...].astype(jnp.float32)
    padded[0:TAPS, :] = taps
    padded[TAPS:, :] = jnp.zeros_like(taps)
    gain[...] = jnp.dot(
        tap[...], taps, precision=lax.Precision.HIGHEST, preferred_element_type=jnp.float32
    )
    for load in loads[:2]:
        load.wait()
    spec[...] = jnp.dot(
        time[:, 0:own_len], own[...], preferred_element_type=jnp.float32
    )

    @pl.when(seg > 0)
    def _():
        forward_copy().wait_recv()

    def seg_copy(slab, slot, target):
        return pltpu.make_async_remote_copy(
            src_ref=outgoing.at[slab, target], dst_ref=held.at[slab, slot],
            send_sem=seg_send.at[slab, target], recv_sem=seg_recv.at[slab, slot],
            device_id={"freq": target}, device_id_type=pl.DeviceIdType.MESH,
        )

    def block(target, cols):
        row = pl.multiple_of(target * bins, bins)
        up, low = pl.ds(row, bins), pl.ds(BINS + row, bins)
        sr, si, gr, gi = spec[up, cols], spec[low, cols], gain[up, cols], gain[low, cols]
        real = sr * gr - si * gi + extra[up, :]
        imag = sr * gi + si * gr + extra[low, :]
        return real.astype(jnp.bfloat16), imag.astype(jnp.bfloat16)

    steps = SHARED // CHUNK // slabs
    for slab in range(slabs):
        cols = slice(slab * LANES, (slab + 1) * LANES)

        @pl.when(seg < segments - 1)
        def _():
            back_copy(slab).wait_recv()

        edge = tail[:, cols].astype(jnp.float32)
        edge = edge - later[slab, SHARED - TAPS :, :].astype(jnp.float32)
        fringe = jnp.zeros_like(edge)
        for e in range(1, TAPS):
            fringe = fringe + padded[e : e + TAPS, cols] * edge[TAPS - e : TAPS - e + 1]
        extra[...] = jnp.dot(
            tap[...], fringe * (1.0 / math.sqrt(DFT_LEN)),
            precision=lax.Precision.HIGHEST, preferred_element_type=jnp.float32,
        )
        spec[:, cols] += jnp.dot(
            time[:, own_len:], later[slab], preferred_element_type=jnp.float32
        )
        for o in order:
            target = lax.rem(me + o, members)
            outgoing[slab, target, 0], outgoing[slab, target, 1] = block(target, cols)
            seg_copy(slab, me, target).start()
        held[slab, me, 0], held[slab, me, 1] = block(me, cols)
        fill_ramps(ramps, dms, me * bins, slab * steps, (slab + 1) * steps)
    fill_matches(matches, units)

    for slab in range(slabs):
        for o in order:
            source = lax.rem(me + o, members)
            seg_copy(slab, source, source).wait_recv()
        channelize(held, twiddle, first, slab)
    loads[2].wait()
    spectra = jnp.dot(
        first[...].astype(jnp.bfloat16), channel[...], preferred_element_type=jnp.float32
    )
    grouped, rest = group_units(spectra, matches, bins)
    real, imag = grouped[:bins], grouped[bins:]
    upper = jnp.concatenate([real, -imag], 1)
    lower = jnp.concatenate([imag, real], 1)
    rows = []
    for at in range(bins):
        left = jnp.concatenate([upper[at : at + 1], lower[at : at + 1]], 0)
        total = jnp.dot(
            left.astype(jnp.bfloat16), ramps[at], preferred_element_type=jnp.float32
        )
        re = total[0:1] + rest[at : at + 1]
        im = total[1:2] + rest[bins + at : bins + at + 1]
        rows.append((re * re + im * im) * (1.0 / CHANNELS))
    turned = jnp.concatenate(rows, 0).T
    for target in range(members):
        power_out[target] = turned[target * kept : (target + 1) * kept]

    def power_copy(slot, target):
        return pltpu.make_async_remote_copy(
            src_ref=power_out.at[target], dst_ref=power_in.at[slot],
            send_sem=pow_send.at[target], recv_sem=pow_recv.at[slot],
            device_id={"freq": target}, device_id_type=pl.DeviceIdType.MESH,
        )

    for o in order:
        power_copy(me, lax.rem(me + o, members)).start()
    power_in[me] = power_out[me]
    for o in order:
        target = lax.rem(me + o, members)
        power_copy(target, target).wait_recv()
    out[...] = jnp.concatenate([power_in[source] for source in range(members)], 1)
    for o in order:
        target = lax.rem(me + o, members)
        for slab in range(slabs):
            seg_copy(slab, target, target).wait_send()
        power_copy(target, target).wait_send()

    @pl.when(seg > 0)
    def _():
        for slab in range(slabs):
            back_copy(slab).wait_send()

    @pl.when(seg < segments - 1)
    def _():
        forward_copy().wait_send()


def body(raw_samples, filter_taps, dm_trials, channel_units):
    members = lax.axis_size("freq")
    own_len, width = raw_samples.shape
    bins, kept, slabs = BINS // members, DMS // members, width // LANES
    time, tap, twiddle, channel = tables()
    units = channel_units.reshape(CHANNELS // LANES, LANES)
    vmem = pl.BlockSpec(memory_space=pltpu.VMEM)
    anywhere = pl.BlockSpec(memory_space=pl.ANY)
    dma = pltpu.SemaphoreType.DMA
    power = pl.pallas_call(
        functools.partial(kernel, members, lax.axis_size("tm")),
        out_shape=pltpu.VMEM((kept, BINS), jnp.float32),
        in_specs=[anywhere] * 3 + [vmem] * 5,
        out_specs=vmem,
        scratch_shapes=[
            pltpu.VMEM((own_len, width), jnp.bfloat16),
            pltpu.VMEM(time.shape, jnp.bfloat16),
            pltpu.VMEM(channel.shape, jnp.bfloat16),
            pltpu.VMEM((width // LANES, SHARED, LANES), jnp.bfloat16),
            pltpu.VMEM((TAPS, width), jnp.bfloat16),
            pltpu.VMEM((2 * TAPS, width), jnp.float32),
            pltpu.VMEM((2 * BINS, width), jnp.float32),
            pltpu.VMEM((2 * BINS, width), jnp.float32),
            pltpu.VMEM((2 * BINS, LANES), jnp.float32),
            pltpu.VMEM((slabs, members, 2, bins, LANES), jnp.bfloat16),
            pltpu.VMEM((slabs, members, 2, bins, LANES), jnp.bfloat16),
            pltpu.VMEM((bins, 2 * SHARED, DMS), jnp.bfloat16),
            pltpu.VMEM((RADIX, INNER, SHARED), jnp.bfloat16),
            pltpu.VMEM((RADIX * bins, 2 * INNER), jnp.float32),
            pltpu.VMEM((members, kept, bins), jnp.float32),
            pltpu.VMEM((members, kept, bins), jnp.float32),
            dma((3,)), dma((1 + slabs,)), dma((1 + slabs,)),
            dma((slabs, members)), dma((slabs, members)), dma((members,)), dma((members,)),
        ],
        compiler_params=pltpu.CompilerParams(
            vmem_limit_bytes=56 * 2**20, collective_id=0, has_side_effects=True
        ),
    )(raw_samples, time, channel, filter_taps, units, dm_trials.reshape(1, DMS), tap, twiddle)
    return power[None]


def solution(mesh):
    in_specs = (P(("beam", "tm"), "freq"), P(None, "freq"), P(), P())
    out_specs = P(("beam", "tm"), "freq", None)
    return jax.shard_map(body, mesh=mesh, in_specs=in_specs, out_specs=out_specs, check_vma=False)
```

```python
import functools
import math

import jax
import jax.numpy as jnp
import numpy as np
from jax import lax
from jax.experimental import pallas as pl
from jax.experimental.pallas import tpu as pltpu
from jax.sharding import PartitionSpec as P

TAPS = 16
DFT_LEN = 2048
BINS = 256
SHARED = 512
DMS = 256
DM_STEPS = 1024
CHANNELS = 4096
RADIX = 8
INNER = CHANNELS // RADIX
CHUNK = 16
LANES = 128
SLAB = 256
KEPT = 160


def band_basis():
    at = np.arange(SHARED)
    diag = ((SHARED - 1) / 2 - at) ** 2 * math.cos(2 * math.pi * BINS / DFT_LEN)
    off = at[1:] * (SHARED - at[1:]) / 2.0
    square = off * off
    low = np.full(KEPT, -float(SHARED * SHARED))
    high = np.full(KEPT, float(SHARED * SHARED))
    wanted = SHARED - np.arange(KEPT)
    for _ in range(70):
        middle = (low + high) / 2
        pivot = diag[0] - middle
        below = (pivot < 0).astype(np.int64)
        for row in range(1, SHARED):
            pivot = np.where(pivot == 0, 1e-30, pivot)
            pivot = diag[row] - middle - square[row - 1] / pivot
            below += pivot < 0
        high = np.where(below >= wanted, middle, high)
        low = np.where(below >= wanted, low, middle)
    value = (low + high) / 2
    down, up = np.zeros((SHARED, KEPT)), np.zeros((SHARED, KEPT))
    down[0], up[-1] = diag[0] - value, diag[-1] - value
    for row in range(1, SHARED):
        down[row] = diag[row] - value - square[row - 1] / down[row - 1]
        back = SHARED - 1 - row
        up[back] = diag[back] - value - square[back] / up[back + 1]
    twist = np.argmin(np.abs(down + up - (diag[:, None] - value)), 0)
    basis = np.zeros((SHARED, KEPT))
    basis[twist, np.arange(KEPT)] = 1.0
    for row in range(1, SHARED):
        basis[row] = np.where(row > twist, -off[row - 1] * basis[row - 1] / up[row], basis[row])
        back = SHARED - 1 - row
        step = -off[back] * basis[back + 1] / down[back]
        basis[back] = np.where(back < twist, step, basis[back])
    total = np.zeros(KEPT)
    for row in range(SHARED):
        total = total + basis[row] * basis[row]
    return (basis / np.sqrt(total)).T


def split(values, count):
    parts = []
    for _ in range(count):
        part = np.asarray(values).astype(jnp.bfloat16)
        parts.append(part)
        values = values - part.astype(np.float64)
    return parts


def tables():
    bins = np.arange(BINS)[:, None]
    angle = 2 * np.pi * (bins * np.arange(DFT_LEN)[None, :] % DFT_LEN) / DFT_LEN
    time = np.concatenate([np.cos(angle), -np.sin(angle)], 0) / math.sqrt(DFT_LEN)
    basis = band_basis()
    shrink = np.concatenate(split(basis, 2), 0)
    grow = np.concatenate(split(np.dot(time[:, DFT_LEN - SHARED :], basis.T), 2), 1)
    angle = 2 * np.pi * (bins * np.arange(TAPS)[None, :]) / DFT_LEN
    tap = split(np.concatenate([np.cos(angle), -np.sin(angle)], 0), 3)
    tap = np.concatenate([tap[0], tap[1], tap[2], tap[0], tap[1], tap[0]], 1)
    ids = np.arange(INNER)
    angle = 2 * np.pi * (np.arange(RADIX)[:, None] * ids[None, :]) / CHANNELS
    twiddle = np.stack([np.cos(angle), -np.sin(angle)]) / math.sqrt(RADIX)
    spread = ids.reshape(CHANNELS // LANES, LANES // RADIX).T.reshape(-1)
    angle = 2 * np.pi * (ids[:, None] * spread[None, :] % INNER) / INNER
    cosine, sine = np.cos(angle), np.sin(angle)
    channel = np.block([[cosine, -sine], [sine, cosine]]) / math.sqrt(INNER)
    return (
        jnp.asarray(time[:, : DFT_LEN - SHARED], jnp.bfloat16),
        jnp.asarray(channel, jnp.bfloat16),
        jnp.asarray(shrink),
        jnp.asarray(grow),
        jnp.asarray(tap),
        jnp.asarray(twiddle, jnp.float32),
    )


def unit_circle(phase):
    x = phase.astype(jnp.float32) * (2.0 * math.pi / DFT_LEN)
    y = x * x
    sine, cosine = jnp.full_like(y, -1 / 39916800), jnp.full_like(y, 1 / 479001600)
    for value in (1 / 362880, -1 / 5040, 1 / 120, -1 / 6, 1.0):
        sine = sine * y + value
    for value in (-1 / 3628800, 1 / 40320, -1 / 720, 1 / 24, -0.5, 1.0):
        cosine = cosine * y + value
    return cosine, sine * x


def fill_ramps(ramps, dms, first_bin, start, stop):
    bins = ramps.shape[0]

    @pl.loop(start, stop)
    def _(step):
        row = pl.multiple_of(step * CHUNK, CHUNK)
        units = lax.broadcasted_iota(jnp.int32, (CHUNK, DMS), 0) + (row + 1)
        delays = (units * dms[...]) >> 10
        turn_cos, turn_sin = unit_circle(delays)
        phase = (delays * first_bin) & (DFT_LEN - 1)
        quarter = phase >> 9
        cosine, sine = unit_circle(phase & 511)
        odd = (quarter & 1) == 1
        swapped_cos = jnp.where(odd, -sine, cosine)
        swapped_sin = jnp.where(odd, cosine, sine)
        far = quarter >= 2
        cosine = jnp.where(far, -swapped_cos, swapped_cos)
        sine = jnp.where(far, -swapped_sin, swapped_sin)
        for at in range(bins):
            ramps[at, pl.ds(row, CHUNK), :] = cosine.astype(jnp.bfloat16)
            ramps[at, pl.ds(SHARED + row, CHUNK), :] = sine.astype(jnp.bfloat16)
            if at + 1 < bins:
                cosine, sine = (
                    cosine * turn_cos - sine * turn_sin,
                    sine * turn_cos + cosine * turn_sin,
                )


def dft(real, imag):
    count = len(real)
    if count == 1:
        return real, imag
    er, ei = dft(real[0::2], imag[0::2])
    odr, odi = dft(real[1::2], imag[1::2])
    half = count // 2
    outs = [None] * count
    for k in range(half):
        if k == 0:
            tr, ti = odr[k], odi[k]
        elif 4 * k == count:
            tr, ti = odi[k], -odr[k]
        else:
            c, s = math.cos(2 * math.pi * k / count), math.sin(2 * math.pi * k / count)
            tr, ti = odr[k] * c + odi[k] * s, odi[k] * c - odr[k] * s
        outs[k] = (er[k] + tr, ei[k] + ti)
        outs[k + half] = (er[k] - tr, ei[k] - ti)
    return [o[0] for o in outs], [o[1] for o in outs]


def channelize(held, twiddle, first, slab):
    slabs, members, _, bins, wide = held.shape
    per = members // RADIX
    for src in range(per):
        lane = src * slabs + slab
        real, imag = [], []
        for n2 in range(RADIX):
            real.append(held[slab, n2 * per + src, 0].astype(jnp.float32))
            imag.append(held[slab, n2 * per + src, 1].astype(jnp.float32))
        real, imag = dft(real, imag)
        cols = slice(lane * wide, lane * wide + wide)
        cols_imag = slice(INNER + lane * wide, INNER + lane * wide + wide)
        for k2 in range(RADIX):
            c, s = twiddle[0, k2 : k2 + 1, cols], twiddle[1, k2 : k2 + 1, cols]
            rows = slice(k2 * bins, k2 * bins + bins)
            first[rows, cols] = real[k2] * c - imag[k2] * s
            first[rows, cols_imag] = real[k2] * s + imag[k2] * c


def fill_matches(matches, units):
    rows, lanes = units.shape
    ids = lax.broadcasted_iota(jnp.int32, (rows, SHARED), 1) + 1
    for k2 in range(RADIX):
        for at in range(lanes // RADIX):
            lane = at * RADIX + k2
            same = (units[:, lane : lane + 1] == ids).astype(jnp.float32)
            matches[k2, at * rows : (at + 1) * rows, :] = same.astype(jnp.bfloat16)


def group_units(spectra, matches, bins):
    grouped = jnp.zeros((2 * bins, SHARED), jnp.float32)
    whole = jnp.zeros((2 * bins, INNER), jnp.float32)
    for k2 in range(RADIX):
        part = spectra[k2 * bins : (k2 + 1) * bins]
        part = jnp.concatenate([part[:, :INNER], part[:, INNER:]], 0)
        part = part.astype(jnp.bfloat16)
        whole += part.astype(jnp.float32)
        grouped += jnp.dot(part, matches[k2], preferred_element_type=jnp.float32)
    rest = jnp.sum(whole, 1, keepdims=True) - jnp.sum(grouped, 1, keepdims=True)
    return grouped, rest


def partner_order(members):
    return sorted(range(1, members), key=lambda o: -abs(o - members // 2))


def kernel(
    members, segments,
    raw, time_hbm, channel_hbm, shrink_hbm, grow_hbm, filter_taps, units, dms, tap, twiddle,
    out,
    own, time, channel, shrink, grow, edges, later, tail, padded, spec, gain, extra,
    outgoing, held, ramps, matches, first, power_out, power_in,
    local_sem, halo_send, halo_recv, seg_send, seg_recv, pow_send, pow_recv,
):
    me = lax.axis_index("freq")
    seg = lax.axis_index("tm")
    own_len, width = own.shape
    bins = BINS // members
    kept = DMS // members
    slabs, _, wide = later.shape
    head, rest = pl.ds(0, SHARED), pl.ds(SHARED, own_len - SHARED)
    loads = [
        pltpu.make_async_copy(raw.at[head], own.at[head], local_sem.at[0]),
        pltpu.make_async_copy(shrink_hbm, shrink, local_sem.at[1]),
        pltpu.make_async_copy(raw.at[rest], own.at[rest], local_sem.at[2]),
        pltpu.make_async_copy(time_hbm, time, local_sem.at[3]),
        pltpu.make_async_copy(grow_hbm, grow, local_sem.at[4]),
        pltpu.make_async_copy(channel_hbm, channel, local_sem.at[5]),
    ]
    for load in loads:
        load.start()

    barrier = pltpu.get_barrier_semaphore()
    order = partner_order(members)
    for o in order:
        pl.semaphore_signal(
            barrier, inc=1, device_id={"freq": lax.rem(me + o, members)},
            device_id_type=pl.DeviceIdType.MESH,
        )

    @pl.when(seg > 0)
    def _():
        pl.semaphore_signal(
            barrier, inc=1, device_id={"tm": seg - 1}, device_id_type=pl.DeviceIdType.MESH
        )

    @pl.when(seg < segments - 1)
    def _():
        pl.semaphore_signal(
            barrier, inc=1, device_id={"tm": seg + 1}, device_id_type=pl.DeviceIdType.MESH
        )

    for load in loads[:2]:
        load.wait()

    @pl.when(seg > 0)
    def _():
        both = jnp.dot(shrink[...], own[0:SHARED, :], preferred_element_type=jnp.float32)
        both = (both[:KEPT] + both[KEPT:]).astype(jnp.bfloat16)
        for slab in range(slabs):
            cols = slice(slab * wide, (slab + 1) * wide)
            edges[slab, 0:KEPT, :] = both[:, cols]
            edges[slab, KEPT:, :] = own[SHARED - TAPS : SHARED, cols]

    pl.semaphore_wait(
        barrier, members - 1 + jnp.minimum(seg, 1) + jnp.minimum(segments - 1 - seg, 1)
    )

    def back_copy(slab):
        return pltpu.make_async_remote_copy(
            src_ref=edges.at[slab], dst_ref=later.at[slab],
            send_sem=halo_send.at[1 + slab], recv_sem=halo_recv.at[1 + slab],
            device_id={"tm": seg - 1}, device_id_type=pl.DeviceIdType.MESH,
        )

    def forward_copy():
        return pltpu.make_async_remote_copy(
            src_ref=raw.at[pl.ds(own_len - TAPS, TAPS)], dst_ref=tail,
            send_sem=halo_send.at[0], recv_sem=halo_recv.at[0],
            device_id={"tm": seg + 1}, device_id_type=pl.DeviceIdType.MESH,
        )

    @pl.when(seg > 0)
    def _():
        for slab in range(slabs):
            back_copy(slab).start()

    @pl.when(seg == 0)
    def _():
        tail[...] = jnp.zeros_like(tail)

    @pl.when(seg < segments - 1)
    def _():
        forward_copy().start()

    @pl.when(seg == segments - 1)
    def _():
        later[...] = jnp.zeros_like(later)

    taps = filter_taps[...]
    padded[0:TAPS, :] = taps.astype(jnp.float32)
    padded[TAPS:, :] = jnp.zeros((TAPS, width), jnp.float32)
    gain[...] = jnp.dot(
        tap[:, 0 : 3 * TAPS], jnp.concatenate([taps] * 3, 0),
        preferred_element_type=jnp.float32,
    )
    for load in loads[2:4]:
        load.wait()
    spec[...] = jnp.dot(time[...], own[...], preferred_element_type=jnp.float32)
    loads[4].wait()
    fill_matches(matches, units)
    fill_ramps(ramps, dms, me * bins, 0, 6)

    @pl.when(seg > 0)
    def _():
        forward_copy().wait_recv()

    def seg_copy(slab, slot, target):
        return pltpu.make_async_remote_copy(
            src_ref=outgoing.at[slab, target], dst_ref=held.at[slab, slot],
            send_sem=seg_send.at[slab, target], recv_sem=seg_recv.at[slab, slot],
            device_id={"freq": target}, device_id_type=pl.DeviceIdType.MESH,
        )

    def block(target, cols):
        row = pl.multiple_of(target * bins, bins)
        up, low = pl.ds(row, bins), pl.ds(BINS + row, bins)
        sr, si, gr, gi = spec[up, cols], spec[low, cols], gain[up, cols], gain[low, cols]
        real = sr * gr - si * gi + extra[up, :]
        imag = sr * gi + si * gr + extra[low, :]
        return real.astype(jnp.bfloat16), imag.astype(jnp.bfloat16)

    for slab in range(slabs):
        cols = slice(slab * wide, (slab + 1) * wide)

        @pl.when(seg < segments - 1)
        def _():
            back_copy(slab).wait_recv()

        edge = tail[:, cols].astype(jnp.float32)
        edge = edge - later[slab, KEPT:, :].astype(jnp.float32)
        fringe = jnp.zeros_like(edge)
        for e in range(1, TAPS):
            fringe = fringe + padded[e : e + TAPS, cols] * edge[TAPS - e : TAPS - e + 1]
        fringe = fringe * (1.0 / math.sqrt(DFT_LEN))
        one = fringe.astype(jnp.bfloat16)
        left = fringe - one.astype(jnp.float32)
        two = left.astype(jnp.bfloat16)
        three = (left - two.astype(jnp.float32)).astype(jnp.bfloat16)
        extra[...] = jnp.dot(
            tap[...], jnp.concatenate([one, one, one, two, two, three], 0),
            preferred_element_type=jnp.float32,
        )
        spec[:, cols] += jnp.dot(
            grow[...], jnp.concatenate([later[slab, 0:KEPT, :]] * 2, 0),
            preferred_element_type=jnp.float32,
        )
        for o in order:
            target = lax.rem(me + o, members)
            outgoing[slab, target, 0], outgoing[slab, target, 1] = block(target, cols)
            seg_copy(slab, me, target).start()
        held[slab, me, 0], held[slab, me, 1] = block(me, cols)
        if slab + 1 < slabs:
            fill_ramps(ramps, dms, me * bins, 6, 10)
    fill_ramps(ramps, dms, me * bins, 10 if slabs > 1 else 6, SHARED // CHUNK)

    for slab in range(slabs):
        for o in order:
            source = lax.rem(me + o, members)
            seg_copy(slab, source, source).wait_recv()
        channelize(held, twiddle, first, slab)
    loads[5].wait()
    spectra = jnp.dot(
        first[...].astype(jnp.bfloat16), channel[...], preferred_element_type=jnp.float32
    )
    grouped, rest = group_units(spectra, matches, bins)
    real, imag = grouped[:bins], grouped[bins:]
    upper = jnp.concatenate([real, -imag], 1)
    lower = jnp.concatenate([imag, real], 1)
    rows = []
    for at in range(bins):
        left = jnp.concatenate([upper[at : at + 1], lower[at : at + 1]], 0)
        total = jnp.dot(
            left.astype(jnp.bfloat16), ramps[at], preferred_element_type=jnp.float32
        )
        re = total[0:1] + rest[at : at + 1]
        im = total[1:2] + rest[bins + at : bins + at + 1]
        rows.append((re * re + im * im) * (1.0 / CHANNELS))
    turned = jnp.concatenate(rows, 0).T
    for target in range(members):
        power_out[target] = turned[target * kept : (target + 1) * kept]

    def power_copy(slot, target):
        return pltpu.make_async_remote_copy(
            src_ref=power_out.at[target], dst_ref=power_in.at[slot],
            send_sem=pow_send.at[target], recv_sem=pow_recv.at[slot],
            device_id={"freq": target}, device_id_type=pl.DeviceIdType.MESH,
        )

    for o in order:
        power_copy(me, lax.rem(me + o, members)).start()
    power_in[me] = power_out[me]
    for o in order:
        target = lax.rem(me + o, members)
        power_copy(target, target).wait_recv()
    out[...] = jnp.concatenate([power_in[source] for source in range(members)], 1)
    for o in order:
        target = lax.rem(me + o, members)
        for slab in range(slabs):
            seg_copy(slab, target, target).wait_send()
        power_copy(target, target).wait_send()

    @pl.when(seg > 0)
    def _():
        for slab in range(slabs):
            back_copy(slab).wait_send()

    @pl.when(seg < segments - 1)
    def _():
        forward_copy().wait_send()


def body(raw_samples, filter_taps, dm_trials, channel_units):
    members = lax.axis_size("freq")
    own_len, width = raw_samples.shape
    bins, kept, wide = BINS // members, DMS // members, min(SLAB, width)
    slabs, rows = width // wide, KEPT + TAPS
    time, channel, shrink, grow, tap, twiddle = tables()
    units = channel_units.reshape(CHANNELS // LANES, LANES)
    vmem = pl.BlockSpec(memory_space=pltpu.VMEM)
    anywhere = pl.BlockSpec(memory_space=pl.ANY)
    dma = pltpu.SemaphoreType.DMA
    power = pl.pallas_call(
        functools.partial(kernel, members, lax.axis_size("tm")),
        out_shape=pltpu.VMEM((kept, BINS), jnp.float32),
        in_specs=[anywhere] * 5 + [vmem] * 5,
        out_specs=vmem,
        scratch_shapes=[
            pltpu.VMEM((own_len, width), jnp.bfloat16),
            pltpu.VMEM(time.shape, jnp.bfloat16),
            pltpu.VMEM(channel.shape, jnp.bfloat16),
            pltpu.VMEM(shrink.shape, jnp.bfloat16),
            pltpu.VMEM(grow.shape, jnp.bfloat16),
            pltpu.VMEM((slabs, rows, wide), jnp.bfloat16),
            pltpu.VMEM((slabs, rows, wide), jnp.bfloat16),
            pltpu.VMEM((TAPS, width), jnp.bfloat16),
            pltpu.VMEM((2 * TAPS, width), jnp.float32),
            pltpu.VMEM((2 * BINS, width), jnp.float32),
            pltpu.VMEM((2 * BINS, width), jnp.float32),
            pltpu.VMEM((2 * BINS, wide), jnp.float32),
            pltpu.VMEM((slabs, members, 2, bins, wide), jnp.bfloat16),
            pltpu.VMEM((slabs, members, 2, bins, wide), jnp.bfloat16),
            pltpu.VMEM((bins, 2 * SHARED, DMS), jnp.bfloat16),
            pltpu.VMEM((RADIX, INNER, SHARED), jnp.bfloat16),
            pltpu.VMEM((RADIX * bins, 2 * INNER), jnp.float32),
            pltpu.VMEM((members, kept, bins), jnp.float32),
            pltpu.VMEM((members, kept, bins), jnp.float32),
            dma((6,)), dma((1 + slabs,)), dma((1 + slabs,)),
            dma((slabs, members)), dma((slabs, members)), dma((members,)), dma((members,)),
        ],
        compiler_params=pltpu.CompilerParams(
            vmem_limit_bytes=56 * 2**20, collective_id=0, has_side_effects=True
        ),
    )(
        raw_samples, time, channel, shrink, grow,
        filter_taps, units, dm_trials.reshape(1, DMS), tap, twiddle,
    )
    return power[None]


def solution(mesh):
    in_specs = (P(("beam", "tm"), "freq"), P(None, "freq"), P(), P())
    out_specs = P(("beam", "tm"), "freq", None)
    return jax.shard_map(body, mesh=mesh, in_specs=in_specs, out_specs=out_specs, check_vma=False)
```

```python
import functools
import math

import jax
import jax.numpy as jnp
import numpy as np
from jax import lax
from jax.experimental import pallas as pl
from jax.experimental.pallas import tpu as pltpu
from jax.sharding import PartitionSpec as P

TAPS = 16
DFT_LEN = 2048
BINS = 256
SHARED = 512
DMS = 256
DM_STEPS = 1024
CHANNELS = 4096
RADIX = 16
INNER = CHANNELS // RADIX
CHUNK = 16
LANES = 128
SLAB = 256
KEPT = 160


def band_basis():
    at = np.arange(SHARED)
    diag = ((SHARED - 1) / 2 - at) ** 2 * math.cos(2 * math.pi * BINS / DFT_LEN)
    off = at[1:] * (SHARED - at[1:]) / 2.0
    square = off * off
    low = np.full(KEPT, -float(SHARED * SHARED))
    high = np.full(KEPT, float(SHARED * SHARED))
    wanted = SHARED - np.arange(KEPT)
    for _ in range(70):
        middle = (low + high) / 2
        pivot = diag[0] - middle
        below = (pivot < 0).astype(np.int64)
        for row in range(1, SHARED):
            pivot = np.where(pivot == 0, 1e-30, pivot)
            pivot = diag[row] - middle - square[row - 1] / pivot
            below += pivot < 0
        high = np.where(below >= wanted, middle, high)
        low = np.where(below >= wanted, low, middle)
    value = (low + high) / 2
    down, up = np.zeros((SHARED, KEPT)), np.zeros((SHARED, KEPT))
    down[0], up[-1] = diag[0] - value, diag[-1] - value
    for row in range(1, SHARED):
        down[row] = diag[row] - value - square[row - 1] / down[row - 1]
        back = SHARED - 1 - row
        up[back] = diag[back] - value - square[back] / up[back + 1]
    twist = np.argmin(np.abs(down + up - (diag[:, None] - value)), 0)
    basis = np.zeros((SHARED, KEPT))
    basis[twist, np.arange(KEPT)] = 1.0
    for row in range(1, SHARED):
        basis[row] = np.where(row > twist, -off[row - 1] * basis[row - 1] / up[row], basis[row])
        back = SHARED - 1 - row
        step = -off[back] * basis[back + 1] / down[back]
        basis[back] = np.where(back < twist, step, basis[back])
    total = np.zeros(KEPT)
    for row in range(SHARED):
        total = total + basis[row] * basis[row]
    return (basis / np.sqrt(total)).T


def split(values, count):
    parts = []
    for _ in range(count):
        part = np.asarray(values).astype(jnp.bfloat16)
        parts.append(part)
        values = values - part.astype(np.float64)
    return parts


def tables(chips):
    bins = np.arange(BINS)[:, None]
    angle = 2 * np.pi * (bins * np.arange(DFT_LEN)[None, :] % DFT_LEN) / DFT_LEN
    time = np.concatenate([np.cos(angle), -np.sin(angle)], 0) / math.sqrt(DFT_LEN)
    basis = band_basis()
    shrink = np.concatenate(split(basis, 2), 0)
    grow = np.concatenate(split(np.dot(time[:, DFT_LEN - SHARED :], basis.T), 2), 1)
    angle = 2 * np.pi * (bins * np.arange(TAPS)[None, :]) / DFT_LEN
    tap = split(np.concatenate([np.cos(angle), -np.sin(angle)], 0), 3)
    tap = np.concatenate([tap[0], tap[1], tap[2], tap[0], tap[1], tap[0]], 1)
    ids = np.arange(INNER)
    start = (np.arange(chips) * (CHANNELS // chips))[:, None, None]
    angle = np.arange(RADIX)[:, None] * (ids[None, :] + start) % CHANNELS
    angle = 2 * np.pi * angle / CHANNELS
    twiddle = np.stack([np.cos(angle), -np.sin(angle)], 1) / math.sqrt(RADIX)
    spread = ids.reshape(CHANNELS // LANES, LANES // RADIX).T.reshape(-1)
    angle = 2 * np.pi * (ids[:, None] * spread[None, :] % INNER) / INNER
    cosine, sine = np.cos(angle), np.sin(angle)
    channel = np.block([[cosine, -sine], [sine, cosine]]) / math.sqrt(INNER)
    return (
        jnp.asarray(time[:, : DFT_LEN - SHARED], jnp.bfloat16),
        jnp.asarray(channel, jnp.bfloat16),
        jnp.asarray(shrink),
        jnp.asarray(grow),
        jnp.asarray(tap),
        jnp.asarray(twiddle, jnp.float32),
    )


def unit_circle(phase):
    x = phase.astype(jnp.float32) * (2.0 * math.pi / DFT_LEN)
    y = x * x
    sine, cosine = jnp.full_like(y, -1 / 39916800), jnp.full_like(y, 1 / 479001600)
    for value in (1 / 362880, -1 / 5040, 1 / 120, -1 / 6, 1.0):
        sine = sine * y + value
    for value in (-1 / 3628800, 1 / 40320, -1 / 720, 1 / 24, -0.5, 1.0):
        cosine = cosine * y + value
    return cosine, sine * x


def fill_ramps(ramps, dms, first_bin, start, stop):
    bins = ramps.shape[0]

    @pl.loop(start, stop)
    def _(step):
        row = pl.multiple_of(step * CHUNK, CHUNK)
        units = lax.broadcasted_iota(jnp.int32, (CHUNK, DMS), 0) + (row + 1)
        delays = (units * dms[...]) >> 10
        turn_cos, turn_sin = unit_circle(delays)
        phase = (delays * first_bin) & (DFT_LEN - 1)
        quarter = phase >> 9
        cosine, sine = unit_circle(phase & 511)
        odd = (quarter & 1) == 1
        swapped_cos = jnp.where(odd, -sine, cosine)
        swapped_sin = jnp.where(odd, cosine, sine)
        far = quarter >= 2
        cosine = jnp.where(far, -swapped_cos, swapped_cos)
        sine = jnp.where(far, -swapped_sin, swapped_sin)
        for at in range(bins):
            ramps[at, pl.ds(row, CHUNK), :] = cosine.astype(jnp.bfloat16)
            ramps[at, pl.ds(SHARED + row, CHUNK), :] = sine.astype(jnp.bfloat16)
            if at + 1 < bins:
                cosine, sine = (
                    cosine * turn_cos - sine * turn_sin,
                    sine * turn_cos + cosine * turn_sin,
                )


def dft(real, imag):
    count = len(real)
    if count == 1:
        return real, imag
    er, ei = dft(real[0::2], imag[0::2])
    odr, odi = dft(real[1::2], imag[1::2])
    half = count // 2
    outs = [None] * count
    for k in range(half):
        if k == 0:
            tr, ti = odr[k], odi[k]
        elif 4 * k == count:
            tr, ti = odi[k], -odr[k]
        else:
            c, s = math.cos(2 * math.pi * k / count), math.sin(2 * math.pi * k / count)
            tr, ti = odr[k] * c + odi[k] * s, odi[k] * c - odr[k] * s
        outs[k] = (er[k] + tr, ei[k] + ti)
        outs[k + half] = (er[k] - tr, ei[k] - ti)
    return [o[0] for o in outs], [o[1] for o in outs]


def channelize(pair, twiddle, first, chip):
    cores, slabs, _, _, bins, wide = pair.shape
    real, imag = [], []
    for core in range(cores):
        for slab in range(slabs):
            real.append(pair[core, slab, 0, chip].astype(jnp.float32))
            imag.append(pair[core, slab, 1, chip].astype(jnp.float32))
    join = max(1, INNER // wide)
    real = [jnp.concatenate(real[at : at + join], 1) for at in range(0, len(real), join)]
    imag = [jnp.concatenate(imag[at : at + join], 1) for at in range(0, len(imag), join)]
    fold = len(real)
    stride = RADIX // fold
    for r in range(stride):
        turned_real, turned_imag = [], []
        for f in range(fold):
            c, s = math.cos(2 * math.pi * r * f / RADIX), math.sin(2 * math.pi * r * f / RADIX)
            if r * f == 0:
                turned_real.append(real[f])
                turned_imag.append(imag[f])
            else:
                turned_real.append(real[f] * c + imag[f] * s)
                turned_imag.append(imag[f] * c - real[f] * s)
        outs_real, outs_imag = dft(turned_real, turned_imag)
        for at in range(fold):
            k2 = r + stride * at
            c, s = twiddle[0, k2 : k2 + 1, :], twiddle[1, k2 : k2 + 1, :]
            rows = slice(k2 * bins, k2 * bins + bins)
            first[rows, 0:INNER] = outs_real[at] * c - outs_imag[at] * s
            first[rows, INNER:] = outs_real[at] * s + outs_imag[at] * c


def fill_matches(matches, units):
    rows, lanes = units.shape
    ids = lax.broadcasted_iota(jnp.int32, (rows, SHARED), 1) + 1
    for k2 in range(RADIX):
        for at in range(lanes // RADIX):
            lane = at * RADIX + k2
            same = (units[:, lane : lane + 1] == ids).astype(jnp.float32)
            matches[k2, at * rows : (at + 1) * rows, :] = same.astype(jnp.bfloat16)


def group_units(spectra, matches, bins):
    grouped = jnp.zeros((2 * bins, SHARED), jnp.float32)
    whole = jnp.zeros((2 * bins, INNER), jnp.float32)
    for k2 in range(RADIX):
        part = spectra[k2 * bins : (k2 + 1) * bins]
        part = jnp.concatenate([part[:, :INNER], part[:, INNER:]], 0)
        part = part.astype(jnp.bfloat16)
        whole += part.astype(jnp.float32)
        grouped += jnp.dot(part, matches[k2], preferred_element_type=jnp.float32)
    rest = jnp.sum(whole, 1, keepdims=True) - jnp.sum(grouped, 1, keepdims=True)
    return grouped, rest


def partner_order(members):
    return sorted(range(1, members), key=lambda o: -abs(o - members // 2))


def kernel(
    members, segments,
    raw, time_hbm, channel_hbm, shrink_hbm, grow_hbm, twiddle_hbm,
    filter_taps, units, dms, tap,
    out,
    own, time, channel, shrink, grow, twiddle, edges, later, tail, padded, spec, gain, extra,
    halves, pair, ramps, matches, first, sums_out, sums_in, power_out, power_in,
    local_sem, halo_send, halo_recv, pair_send, pair_recv, sum_send, sum_recv,
    pow_send, pow_recv,
):
    me = lax.axis_index("freq")
    seg = lax.axis_index("tm")
    chips = members // 2
    chip, core = me // 2, me % 2
    own_len, width = own.shape
    bins = BINS // members
    kept = DMS // members
    slabs, _, wide = later.shape
    head, rest = pl.ds(0, SHARED), pl.ds(SHARED, own_len - SHARED)
    loads = [
        pltpu.make_async_copy(raw.at[head], own.at[head], local_sem.at[0]),
        pltpu.make_async_copy(shrink_hbm, shrink, local_sem.at[1]),
        pltpu.make_async_copy(raw.at[rest], own.at[rest], local_sem.at[2]),
        pltpu.make_async_copy(time_hbm, time, local_sem.at[3]),
        pltpu.make_async_copy(grow_hbm, grow, local_sem.at[4]),
        pltpu.make_async_copy(channel_hbm, channel, local_sem.at[5]),
        pltpu.make_async_copy(twiddle_hbm.at[chip], twiddle, local_sem.at[6]),
    ]
    for load in loads:
        load.start()

    barrier = pltpu.get_barrier_semaphore()
    order = partner_order(members)
    for o in order:
        pl.semaphore_signal(
            barrier, inc=1, device_id={"freq": lax.rem(me + o, members)},
            device_id_type=pl.DeviceIdType.MESH,
        )

    @pl.when(seg > 0)
    def _():
        pl.semaphore_signal(
            barrier, inc=1, device_id={"tm": seg - 1}, device_id_type=pl.DeviceIdType.MESH
        )

    @pl.when(seg < segments - 1)
    def _():
        pl.semaphore_signal(
            barrier, inc=1, device_id={"tm": seg + 1}, device_id_type=pl.DeviceIdType.MESH
        )

    for load in loads[:2]:
        load.wait()

    @pl.when(seg > 0)
    def _():
        both = jnp.dot(shrink[...], own[0:SHARED, :], preferred_element_type=jnp.float32)
        both = (both[:KEPT] + both[KEPT:]).astype(jnp.bfloat16)
        for slab in range(slabs):
            cols = slice(slab * wide, (slab + 1) * wide)
            edges[slab, 0:KEPT, :] = both[:, cols]
            edges[slab, KEPT:, :] = own[SHARED - TAPS : SHARED, cols]

    pl.semaphore_wait(
        barrier, members - 1 + jnp.minimum(seg, 1) + jnp.minimum(segments - 1 - seg, 1)
    )

    def back_copy(slab):
        return pltpu.make_async_remote_copy(
            src_ref=edges.at[slab], dst_ref=later.at[slab],
            send_sem=halo_send.at[1 + slab], recv_sem=halo_recv.at[1 + slab],
            device_id={"tm": seg - 1}, device_id_type=pl.DeviceIdType.MESH,
        )

    def forward_copy():
        return pltpu.make_async_remote_copy(
            src_ref=raw.at[pl.ds(own_len - TAPS, TAPS)], dst_ref=tail,
            send_sem=halo_send.at[0], recv_sem=halo_recv.at[0],
            device_id={"tm": seg + 1}, device_id_type=pl.DeviceIdType.MESH,
        )

    @pl.when(seg > 0)
    def _():
        for slab in range(slabs):
            back_copy(slab).start()

    @pl.when(seg == 0)
    def _():
        tail[...] = jnp.zeros_like(tail)

    @pl.when(seg < segments - 1)
    def _():
        forward_copy().start()

    @pl.when(seg == segments - 1)
    def _():
        later[...] = jnp.zeros_like(later)

    taps = filter_taps[...]
    padded[0:TAPS, :] = taps.astype(jnp.float32)
    padded[TAPS:, :] = jnp.zeros((TAPS, width), jnp.float32)
    gain[...] = jnp.dot(
        tap[:, 0 : 3 * TAPS], jnp.concatenate([taps] * 3, 0),
        preferred_element_type=jnp.float32,
    )
    for load in loads[2:4]:
        load.wait()
    spec[...] = jnp.dot(time[...], own[...], preferred_element_type=jnp.float32)
    loads[4].wait()
    fill_matches(matches, units)
    first_bin = core * (BINS // 2) + chip * bins
    fill_ramps(ramps, dms, first_bin, 0, 8)

    @pl.when(seg > 0)
    def _():
        forward_copy().wait_recv()

    def pair_copy(slab):
        return pltpu.make_async_remote_copy(
            src_ref=halves.at[slab], dst_ref=pair.at[core, slab],
            send_sem=pair_send.at[slab], recv_sem=pair_recv.at[slab],
            device_id={"freq": me + 1 - 2 * core}, device_id_type=pl.DeviceIdType.MESH,
        )

    def block(half, at, cols):
        row = pl.multiple_of(half * (BINS // 2) + at * bins, bins)
        up, low = pl.ds(row, bins), pl.ds(BINS + row, bins)
        sr, si, gr, gi = spec[up, cols], spec[low, cols], gain[up, cols], gain[low, cols]
        real = sr * gr - si * gi + extra[up, :]
        imag = sr * gi + si * gr + extra[low, :]
        return real.astype(jnp.bfloat16), imag.astype(jnp.bfloat16)

    for slab in range(slabs):
        cols = slice(slab * wide, (slab + 1) * wide)

        @pl.when(seg < segments - 1)
        def _():
            back_copy(slab).wait_recv()

        edge = tail[:, cols].astype(jnp.float32)
        edge = edge - later[slab, KEPT:, :].astype(jnp.float32)
        fringe = jnp.zeros_like(edge)
        for e in range(1, TAPS):
            fringe = fringe + padded[e : e + TAPS, cols] * edge[TAPS - e : TAPS - e + 1]
        fringe = fringe * (1.0 / math.sqrt(DFT_LEN))
        one = fringe.astype(jnp.bfloat16)
        left = fringe - one.astype(jnp.float32)
        two = left.astype(jnp.bfloat16)
        three = (left - two.astype(jnp.float32)).astype(jnp.bfloat16)
        extra[...] = jnp.dot(
            tap[...], jnp.concatenate([one, one, one, two, two, three], 0),
            preferred_element_type=jnp.float32,
        )
        spec[:, cols] += jnp.dot(
            grow[...], jnp.concatenate([later[slab, 0:KEPT, :]] * 2, 0),
            preferred_element_type=jnp.float32,
        )
        for at in range(chips):
            halves[slab, 0, at], halves[slab, 1, at] = block(1 - core, at, cols)
        pair_copy(slab).start()
        for at in range(chips):
            pair[core, slab, 0, at], pair[core, slab, 1, at] = block(core, at, cols)
    fill_ramps(ramps, dms, first_bin, 8, 12)
    for load in loads[5:]:
        load.wait()
    for slab in range(slabs):
        pair_copy(slab).wait_recv()

    def sum_copy(slot, target):
        return pltpu.make_async_remote_copy(
            src_ref=sums_out.at[target], dst_ref=sums_in.at[slot],
            send_sem=sum_send.at[target], recv_sem=sum_recv.at[slot],
            device_id={"freq": 2 * target + core}, device_id_type=pl.DeviceIdType.MESH,
        )

    def partial(at):
        channelize(pair, twiddle, first, at)
        spectra = jnp.dot(
            first[...].astype(jnp.bfloat16), channel[...], preferred_element_type=jnp.float32
        )
        return group_units(spectra, matches, bins)

    ones = lax.broadcasted_iota(jnp.int32, (2 * bins, LANES), 0)
    ones = (ones == lax.broadcasted_iota(jnp.int32, (2 * bins, LANES), 1)).astype(jnp.float32)
    blocks = SHARED // LANES
    hops = partner_order(chips)[::-1]
    for o in hops:
        target = lax.rem(chip + o, chips)
        grouped, rest = partial(target)
        line = jnp.sum(rest * ones, 0, keepdims=True)
        high = line.astype(jnp.bfloat16).astype(jnp.float32)
        row = lax.broadcasted_iota(jnp.int32, (TAPS, LANES), 0)
        lines = jnp.where(row == 0, high, jnp.where(row == 1, line - high, 0.0))
        pieces = [grouped[:, at * LANES : (at + 1) * LANES] for at in range(blocks)]
        sums_out[target] = jnp.concatenate(pieces + [lines], 0).astype(jnp.bfloat16)
        sum_copy(chip, target).start()
    grouped, rest = partial(chip)
    fill_ramps(ramps, dms, first_bin, 12, SHARED // CHUNK)
    for o in hops:
        source = lax.rem(chip + o, chips)
        sum_copy(source, source).wait_recv()
        came = sums_in[source].astype(jnp.float32)
        size = 2 * bins
        pieces = [came[at * size : (at + 1) * size] for at in range(blocks)]
        grouped += jnp.concatenate(pieces, 1)
        line = came[blocks * size : blocks * size + 1] + came[blocks * size + 1 : blocks * size + 2]
        rest += jnp.sum(line * ones, 1, keepdims=True)
    real, imag = grouped[:bins], grouped[bins:]
    upper = jnp.concatenate([real, -imag], 1)
    lower = jnp.concatenate([imag, real], 1)
    rows = []
    for at in range(bins):
        left = jnp.concatenate([upper[at : at + 1], lower[at : at + 1]], 0)
        total = jnp.dot(
            left.astype(jnp.bfloat16), ramps[at], preferred_element_type=jnp.float32
        )
        re = total[0:1] + rest[at : at + 1]
        im = total[1:2] + rest[bins + at : bins + at + 1]
        rows.append((re * re + im * im) * (1.0 / CHANNELS))
    turned = jnp.concatenate(rows, 0).T
    for target in range(members):
        power_out[target] = turned[target * kept : (target + 1) * kept]

    def power_copy(slot, target):
        return pltpu.make_async_remote_copy(
            src_ref=power_out.at[target], dst_ref=power_in.at[slot],
            send_sem=pow_send.at[target], recv_sem=pow_recv.at[slot],
            device_id={"freq": target}, device_id_type=pl.DeviceIdType.MESH,
        )

    for o in order:
        power_copy(me, lax.rem(me + o, members)).start()
    power_in[me] = power_out[me]
    for o in order:
        target = lax.rem(me + o, members)
        power_copy(target, target).wait_recv()
    sources = [2 * at + half for half in range(2) for at in range(chips)]
    out[...] = jnp.concatenate([power_in[source] for source in sources], 1)
    for o in order:
        target = lax.rem(me + o, members)
        power_copy(target, target).wait_send()
    for slab in range(slabs):
        pair_copy(slab).wait_send()
    for o in hops:
        target = lax.rem(chip + o, chips)
        sum_copy(target, target).wait_send()

    @pl.when(seg > 0)
    def _():
        for slab in range(slabs):
            back_copy(slab).wait_send()

    @pl.when(seg < segments - 1)
    def _():
        forward_copy().wait_send()


def body(raw_samples, filter_taps, dm_trials, channel_units):
    members = lax.axis_size("freq")
    own_len, width = raw_samples.shape
    bins, kept, wide = BINS // members, DMS // members, min(SLAB, width)
    slabs, rows = width // wide, KEPT + TAPS
    swap = 2 * bins * (SHARED // LANES) + TAPS
    chips = members // 2
    time, channel, shrink, grow, tap, twiddle = tables(chips)
    units = channel_units.reshape(CHANNELS // LANES, LANES)
    vmem = pl.BlockSpec(memory_space=pltpu.VMEM)
    anywhere = pl.BlockSpec(memory_space=pl.ANY)
    dma = pltpu.SemaphoreType.DMA
    power = pl.pallas_call(
        functools.partial(kernel, members, lax.axis_size("tm")),
        out_shape=pltpu.VMEM((kept, BINS), jnp.float32),
        in_specs=[anywhere] * 6 + [vmem] * 4,
        out_specs=vmem,
        scratch_shapes=[
            pltpu.VMEM((own_len, width), jnp.bfloat16),
            pltpu.VMEM(time.shape, jnp.bfloat16),
            pltpu.VMEM(channel.shape, jnp.bfloat16),
            pltpu.VMEM(shrink.shape, jnp.bfloat16),
            pltpu.VMEM(grow.shape, jnp.bfloat16),
            pltpu.VMEM(twiddle.shape[1:], jnp.float32),
            pltpu.VMEM((slabs, rows, wide), jnp.bfloat16),
            pltpu.VMEM((slabs, rows, wide), jnp.bfloat16),
            pltpu.VMEM((TAPS, width), jnp.bfloat16),
            pltpu.VMEM((2 * TAPS, width), jnp.float32),
            pltpu.VMEM((2 * BINS, width), jnp.float32),
            pltpu.VMEM((2 * BINS, width), jnp.float32),
            pltpu.VMEM((2 * BINS, wide), jnp.float32),
            pltpu.VMEM((slabs, 2, chips, bins, wide), jnp.bfloat16),
            pltpu.VMEM((2, slabs, 2, chips, bins, wide), jnp.bfloat16),
            pltpu.VMEM((bins, 2 * SHARED, DMS), jnp.bfloat16),
            pltpu.VMEM((RADIX, INNER, SHARED), jnp.bfloat16),
            pltpu.VMEM((RADIX * bins, 2 * INNER), jnp.float32),
            pltpu.VMEM((chips, swap, LANES), jnp.bfloat16),
            pltpu.VMEM((chips, swap, LANES), jnp.bfloat16),
            pltpu.VMEM((members, kept, bins), jnp.float32),
            pltpu.VMEM((members, kept, bins), jnp.float32),
            dma((7,)), dma((1 + slabs,)), dma((1 + slabs,)), dma((slabs,)), dma((slabs,)),
            dma((chips,)), dma((chips,)), dma((members,)), dma((members,)),
        ],
        compiler_params=pltpu.CompilerParams(
            vmem_limit_bytes=56 * 2**20, collective_id=0, has_side_effects=True
        ),
    )(
        raw_samples, time, channel, shrink, grow, twiddle,
        filter_taps, units, dm_trials.reshape(1, DMS), tap,
    )
    return power[None]


def solution(mesh):
    in_specs = (P(("beam", "tm"), "freq"), P(None, "freq"), P(), P())
    out_specs = P(("beam", "tm"), "freq", None)
    return jax.shard_map(body, mesh=mesh, in_specs=in_specs, out_specs=out_specs, check_vma=False)
```

```python
import functools
import math

import jax
import jax.numpy as jnp
import numpy as np
from jax import lax
from jax.experimental import pallas as pl
from jax.experimental.pallas import tpu as pltpu
from jax.sharding import PartitionSpec as P

TAPS = 16
DFT_LEN = 2048
BINS = 256
SHARED = 512
DMS = 256
DM_STEPS = 1024
CHANNELS = 4096
RADIX = 16
INNER = CHANNELS // RADIX
CHUNK = 16
LANES = 128
SLAB = 256
KEPT = 160


def band_basis():
    at = np.arange(SHARED)
    diag = ((SHARED - 1) / 2 - at) ** 2 * math.cos(2 * math.pi * BINS / DFT_LEN)
    off = at[1:] * (SHARED - at[1:]) / 2.0
    square = off * off
    low = np.full(KEPT, -float(SHARED * SHARED))
    high = np.full(KEPT, float(SHARED * SHARED))
    wanted = SHARED - np.arange(KEPT)
    for _ in range(70):
        middle = (low + high) / 2
        pivot = diag[0] - middle
        below = (pivot < 0).astype(np.int64)
        for row in range(1, SHARED):
            pivot = np.where(pivot == 0, 1e-30, pivot)
            pivot = diag[row] - middle - square[row - 1] / pivot
            below += pivot < 0
        high = np.where(below >= wanted, middle, high)
        low = np.where(below >= wanted, low, middle)
    value = (low + high) / 2
    down, up = np.zeros((SHARED, KEPT)), np.zeros((SHARED, KEPT))
    down[0], up[-1] = diag[0] - value, diag[-1] - value
    for row in range(1, SHARED):
        down[row] = diag[row] - value - square[row - 1] / down[row - 1]
        back = SHARED - 1 - row
        up[back] = diag[back] - value - square[back] / up[back + 1]
    twist = np.argmin(np.abs(down + up - (diag[:, None] - value)), 0)
    basis = np.zeros((SHARED, KEPT))
    basis[twist, np.arange(KEPT)] = 1.0
    for row in range(1, SHARED):
        basis[row] = np.where(row > twist, -off[row - 1] * basis[row - 1] / up[row], basis[row])
        back = SHARED - 1 - row
        step = -off[back] * basis[back + 1] / down[back]
        basis[back] = np.where(back < twist, step, basis[back])
    total = np.zeros(KEPT)
    for row in range(SHARED):
        total = total + basis[row] * basis[row]
    return (basis / np.sqrt(total)).T


def split(values, count):
    parts = []
    for _ in range(count):
        part = np.asarray(values).astype(jnp.bfloat16)
        parts.append(part)
        values = values - part.astype(np.float64)
    return parts


def tables(chips):
    bins = np.arange(BINS)[:, None]
    angle = 2 * np.pi * (bins * np.arange(DFT_LEN)[None, :] % DFT_LEN) / DFT_LEN
    time = np.concatenate([np.cos(angle), -np.sin(angle)], 0) / math.sqrt(DFT_LEN)
    basis = band_basis()
    shrink = np.concatenate(split(basis, 2), 0)
    grow = np.concatenate(split(np.dot(time[:, DFT_LEN - SHARED :], basis.T), 2), 1)
    angle = 2 * np.pi * (bins * np.arange(TAPS)[None, :]) / DFT_LEN
    tap = split(np.concatenate([np.cos(angle), -np.sin(angle)], 0), 3)
    tap = np.concatenate([tap[0], tap[1], tap[2], tap[0], tap[1], tap[0]], 1)
    ids = np.arange(INNER)
    start = (np.arange(chips) * (CHANNELS // chips))[:, None, None]
    angle = np.arange(RADIX)[:, None] * (ids[None, :] + start) % CHANNELS
    angle = 2 * np.pi * angle / CHANNELS
    twiddle = np.stack([np.cos(angle), -np.sin(angle)], 1) / math.sqrt(RADIX)
    spread = ids.reshape(CHANNELS // LANES, LANES // RADIX).T.reshape(-1)
    angle = 2 * np.pi * (ids[:, None] * spread[None, :] % INNER) / INNER
    cosine, sine = np.cos(angle), np.sin(angle)
    channel = np.block([[cosine, -sine], [sine, cosine]]) / math.sqrt(INNER)
    return (
        jnp.asarray(time[:, : DFT_LEN - SHARED], jnp.bfloat16),
        jnp.asarray(channel, jnp.bfloat16),
        jnp.asarray(shrink),
        jnp.asarray(grow),
        jnp.asarray(tap),
        jnp.asarray(twiddle, jnp.float32),
    )


def unit_circle(phase):
    x = phase.astype(jnp.float32) * (2.0 * math.pi / DFT_LEN)
    y = x * x
    sine, cosine = jnp.full_like(y, -1 / 39916800), jnp.full_like(y, 1 / 479001600)
    for value in (1 / 362880, -1 / 5040, 1 / 120, -1 / 6, 1.0):
        sine = sine * y + value
    for value in (-1 / 3628800, 1 / 40320, -1 / 720, 1 / 24, -0.5, 1.0):
        cosine = cosine * y + value
    return cosine, sine * x


def fill_ramps(ramps, dms, first_bin, start, stop):
    bins = ramps.shape[0]

    @pl.loop(start, stop)
    def _(step):
        row = pl.multiple_of(step * CHUNK, CHUNK)
        units = lax.broadcasted_iota(jnp.int32, (CHUNK, DMS), 0) + (row + 1)
        delays = (units * dms[...]) >> 10
        turn_cos, turn_sin = unit_circle(delays)
        phase = (delays * first_bin) & (DFT_LEN - 1)
        quarter = phase >> 9
        cosine, sine = unit_circle(phase & 511)
        odd = (quarter & 1) == 1
        swapped_cos = jnp.where(odd, -sine, cosine)
        swapped_sin = jnp.where(odd, cosine, sine)
        far = quarter >= 2
        cosine = jnp.where(far, -swapped_cos, swapped_cos)
        sine = jnp.where(far, -swapped_sin, swapped_sin)
        for at in range(bins):
            ramps[at, pl.ds(row, CHUNK), :] = cosine.astype(jnp.bfloat16)
            ramps[at, pl.ds(SHARED + row, CHUNK), :] = sine.astype(jnp.bfloat16)
            if at + 1 < bins:
                cosine, sine = (
                    cosine * turn_cos - sine * turn_sin,
                    sine * turn_cos + cosine * turn_sin,
                )


def dft(real, imag):
    count = len(real)
    if count == 1:
        return real, imag
    er, ei = dft(real[0::2], imag[0::2])
    odr, odi = dft(real[1::2], imag[1::2])
    half = count // 2
    outs = [None] * count
    for k in range(half):
        if k == 0:
            tr, ti = odr[k], odi[k]
        elif 4 * k == count:
            tr, ti = odi[k], -odr[k]
        else:
            c, s = math.cos(2 * math.pi * k / count), math.sin(2 * math.pi * k / count)
            tr, ti = odr[k] * c + odi[k] * s, odi[k] * c - odr[k] * s
        outs[k] = (er[k] + tr, ei[k] + ti)
        outs[k + half] = (er[k] - tr, ei[k] - ti)
    return [o[0] for o in outs], [o[1] for o in outs]


def channelize(pair, twiddle, first, half):
    cores, slabs, _, _, chips, size, wide = pair.shape
    bins = chips * size
    real, imag = [], []
    for core in range(cores):
        for slab in range(slabs):
            real.append(pair[core, slab, half, 0].astype(jnp.float32).reshape(bins, wide))
            imag.append(pair[core, slab, half, 1].astype(jnp.float32).reshape(bins, wide))
    join = max(1, INNER // wide)
    real = [jnp.concatenate(real[at : at + join], 1) for at in range(0, len(real), join)]
    imag = [jnp.concatenate(imag[at : at + join], 1) for at in range(0, len(imag), join)]
    fold = len(real)
    stride = RADIX // fold
    for r in range(stride):
        turned_real, turned_imag = [], []
        for f in range(fold):
            c, s = math.cos(2 * math.pi * r * f / RADIX), math.sin(2 * math.pi * r * f / RADIX)
            if r * f == 0:
                turned_real.append(real[f])
                turned_imag.append(imag[f])
            else:
                turned_real.append(real[f] * c + imag[f] * s)
                turned_imag.append(imag[f] * c - real[f] * s)
        outs_real, outs_imag = dft(turned_real, turned_imag)
        for at in range(fold):
            k2 = r + stride * at
            c, s = twiddle[0, k2 : k2 + 1, :], twiddle[1, k2 : k2 + 1, :]
            rows = slice(k2 * bins, k2 * bins + bins)
            first[rows, 0:INNER] = outs_real[at] * c - outs_imag[at] * s
            first[rows, INNER:] = outs_real[at] * s + outs_imag[at] * c


def fill_matches(matches, units):
    rows, lanes = units.shape
    ids = lax.broadcasted_iota(jnp.int32, (rows, SHARED), 1) + 1
    for k2 in range(RADIX):
        for at in range(lanes // RADIX):
            lane = at * RADIX + k2
            same = (units[:, lane : lane + 1] == ids).astype(jnp.float32)
            matches[k2, at * rows : (at + 1) * rows, :] = same.astype(jnp.bfloat16)


def group_units(spectra, matches, bins):
    grouped = jnp.zeros((2 * bins, SHARED), jnp.float32)
    whole = jnp.zeros((2 * bins, INNER), jnp.float32)
    for k2 in range(RADIX):
        part = spectra[k2 * bins : (k2 + 1) * bins]
        part = jnp.concatenate([part[:, :INNER], part[:, INNER:]], 0)
        part = part.astype(jnp.bfloat16)
        whole += part.astype(jnp.float32)
        grouped += jnp.dot(part, matches[k2], preferred_element_type=jnp.float32)
    rest = jnp.sum(whole, 1, keepdims=True) - jnp.sum(grouped, 1, keepdims=True)
    return grouped, rest


def partner_order(members):
    return sorted(range(1, members), key=lambda o: -abs(o - members // 2))


def kernel(
    members, segments,
    raw, time_hbm, channel_hbm, shrink_hbm, grow_hbm, twiddle_hbm,
    filter_taps, units, dms, tap,
    out,
    own, time, channel, shrink, grow, twiddle, edges, later, tail, padded, spec, gain, extra,
    halves, pair, ramps, matches, first, kept_sums, kept_rest, sums_out, sums_in,
    power_out, power_in,
    local_sem, halo_send, halo_recv, pair_send, pair_recv, sum_send, sum_recv,
    pow_send, pow_recv,
):
    me = lax.axis_index("freq")
    seg = lax.axis_index("tm")
    chips = members // 2
    chip, core = me // 2, me % 2
    own_len, width = own.shape
    bins = BINS // members
    kept = DMS // members
    slabs, _, wide = later.shape
    head, rest = pl.ds(0, SHARED), pl.ds(SHARED, own_len - SHARED)
    loads = [
        pltpu.make_async_copy(raw.at[head], own.at[head], local_sem.at[0]),
        pltpu.make_async_copy(shrink_hbm, shrink, local_sem.at[1]),
        pltpu.make_async_copy(raw.at[rest], own.at[rest], local_sem.at[2]),
        pltpu.make_async_copy(time_hbm, time, local_sem.at[3]),
        pltpu.make_async_copy(grow_hbm, grow, local_sem.at[4]),
        pltpu.make_async_copy(channel_hbm, channel, local_sem.at[5]),
        pltpu.make_async_copy(twiddle_hbm.at[chip], twiddle, local_sem.at[6]),
    ]
    for load in loads:
        load.start()

    barrier = pltpu.get_barrier_semaphore()
    order = partner_order(members)
    for o in order:
        pl.semaphore_signal(
            barrier, inc=1, device_id={"freq": lax.rem(me + o, members)},
            device_id_type=pl.DeviceIdType.MESH,
        )

    @pl.when(seg > 0)
    def _():
        pl.semaphore_signal(
            barrier, inc=1, device_id={"tm": seg - 1}, device_id_type=pl.DeviceIdType.MESH
        )

    @pl.when(seg < segments - 1)
    def _():
        pl.semaphore_signal(
            barrier, inc=1, device_id={"tm": seg + 1}, device_id_type=pl.DeviceIdType.MESH
        )

    for load in loads[:2]:
        load.wait()

    @pl.when(seg > 0)
    def _():
        both = jnp.dot(shrink[...], own[0:SHARED, :], preferred_element_type=jnp.float32)
        both = (both[:KEPT] + both[KEPT:]).astype(jnp.bfloat16)
        for slab in range(slabs):
            cols = slice(slab * wide, (slab + 1) * wide)
            edges[slab, 0:KEPT, :] = both[:, cols]
            edges[slab, KEPT:, :] = own[SHARED - TAPS : SHARED, cols]

    pl.semaphore_wait(
        barrier, members - 1 + jnp.minimum(seg, 1) + jnp.minimum(segments - 1 - seg, 1)
    )

    def back_copy(slab):
        return pltpu.make_async_remote_copy(
            src_ref=edges.at[slab], dst_ref=later.at[slab],
            send_sem=halo_send.at[1 + slab], recv_sem=halo_recv.at[1 + slab],
            device_id={"tm": seg - 1}, device_id_type=pl.DeviceIdType.MESH,
        )

    def forward_copy():
        return pltpu.make_async_remote_copy(
            src_ref=raw.at[pl.ds(own_len - TAPS, TAPS)], dst_ref=tail,
            send_sem=halo_send.at[0], recv_sem=halo_recv.at[0],
            device_id={"tm": seg + 1}, device_id_type=pl.DeviceIdType.MESH,
        )

    @pl.when(seg > 0)
    def _():
        for slab in range(slabs):
            back_copy(slab).start()

    @pl.when(seg == 0)
    def _():
        tail[...] = jnp.zeros_like(tail)

    @pl.when(seg < segments - 1)
    def _():
        forward_copy().start()

    @pl.when(seg == segments - 1)
    def _():
        later[...] = jnp.zeros_like(later)

    taps = filter_taps[...]
    padded[0:TAPS, :] = taps.astype(jnp.float32)
    padded[TAPS:, :] = jnp.zeros((TAPS, width), jnp.float32)
    gain[...] = jnp.dot(
        tap[:, 0 : 3 * TAPS], jnp.concatenate([taps] * 3, 0),
        preferred_element_type=jnp.float32,
    )
    for load in loads[2:4]:
        load.wait()
    spec[...] = jnp.dot(time[...], own[...], preferred_element_type=jnp.float32)
    loads[4].wait()
    fill_matches(matches, units)
    first_bin = core * (BINS // 2) + chip * bins
    fill_ramps(ramps, dms, first_bin, 0, 4)

    @pl.when(seg > 0)
    def _():
        forward_copy().wait_recv()

    _, _, parts, _, _, size, _ = pair.shape

    def pair_copy(slab, part):
        return pltpu.make_async_remote_copy(
            src_ref=halves.at[slab, part], dst_ref=pair.at[core, slab, part],
            send_sem=pair_send.at[slab, part], recv_sem=pair_recv.at[slab, part],
            device_id={"freq": me + 1 - 2 * core}, device_id_type=pl.DeviceIdType.MESH,
        )

    def block(half, part, at, cols):
        row = pl.multiple_of(half * (BINS // 2) + at * bins + part * size, size)
        up, low = pl.ds(row, size), pl.ds(BINS + row, size)
        sr, si, gr, gi = spec[up, cols], spec[low, cols], gain[up, cols], gain[low, cols]
        real = sr * gr - si * gi + extra[up, :]
        imag = sr * gi + si * gr + extra[low, :]
        return real.astype(jnp.bfloat16), imag.astype(jnp.bfloat16)

    for slab in range(slabs):
        cols = slice(slab * wide, (slab + 1) * wide)

        @pl.when(seg < segments - 1)
        def _():
            back_copy(slab).wait_recv()

        edge = tail[:, cols].astype(jnp.float32)
        edge = edge - later[slab, KEPT:, :].astype(jnp.float32)
        fringe = jnp.zeros_like(edge)
        for e in range(1, TAPS):
            fringe = fringe + padded[e : e + TAPS, cols] * edge[TAPS - e : TAPS - e + 1]
        fringe = fringe * (1.0 / math.sqrt(DFT_LEN))
        one = fringe.astype(jnp.bfloat16)
        left = fringe - one.astype(jnp.float32)
        two = left.astype(jnp.bfloat16)
        three = (left - two.astype(jnp.float32)).astype(jnp.bfloat16)
        extra[...] = jnp.dot(
            tap[...], jnp.concatenate([one, one, one, two, two, three], 0),
            preferred_element_type=jnp.float32,
        )
        spec[:, cols] += jnp.dot(
            grow[...], jnp.concatenate([later[slab, 0:KEPT, :]] * 2, 0),
            preferred_element_type=jnp.float32,
        )
        for part in range(parts):
            for at in range(chips):
                real, imag = block(1 - core, part, at, cols)
                halves[slab, part, 0, at], halves[slab, part, 1, at] = real, imag
            pair_copy(slab, part).start()
        for part in range(parts):
            for at in range(chips):
                real, imag = block(core, part, at, cols)
                pair[core, slab, part, 0, at], pair[core, slab, part, 1, at] = real, imag
        if slab + 1 < slabs:
            fill_ramps(ramps, dms, first_bin, 4, 8)
    fill_ramps(ramps, dms, first_bin, 8 if slabs > 1 else 4, 10)
    for load in loads[5:]:
        load.wait()

    def sum_copy(part, slot, target):
        return pltpu.make_async_remote_copy(
            src_ref=sums_out.at[part, target], dst_ref=sums_in.at[part, slot],
            send_sem=sum_send.at[part, target], recv_sem=sum_recv.at[part, slot],
            device_id={"freq": 2 * target + core}, device_id_type=pl.DeviceIdType.MESH,
        )

    ones = lax.broadcasted_iota(jnp.int32, (2 * size, LANES), 0)
    ones = (ones == lax.broadcasted_iota(jnp.int32, (2 * size, LANES), 1)).astype(jnp.float32)
    blocks = SHARED // LANES
    hops = partner_order(chips)[::-1]
    some = chips * size
    for part in range(parts):
        for slab in range(slabs):
            pair_copy(slab, part).wait_recv()
        channelize(pair, twiddle, first, part)
        spectra = jnp.dot(
            first[...].astype(jnp.bfloat16), channel[...], preferred_element_type=jnp.float32
        )
        grouped, rest = group_units(spectra, matches, some)
        for at in range(chips):
            up, low = slice(at * size, (at + 1) * size), slice(some + at * size, some + (at + 1) * size)
            own_sums = jnp.concatenate([grouped[up], grouped[low]], 0)
            own_rest = jnp.concatenate([rest[up], rest[low]], 0)
            kept_sums[part, at] = own_sums
            kept_rest[part, at] = jnp.broadcast_to(own_rest, (2 * size, LANES))
            line = jnp.sum(own_rest * ones, 0, keepdims=True)
            high = line.astype(jnp.bfloat16).astype(jnp.float32)
            row = lax.broadcasted_iota(jnp.int32, (TAPS, LANES), 0)
            lines = jnp.where(row == 0, high, jnp.where(row == 1, line - high, 0.0))
            pieces = [own_sums[:, lane * LANES : (lane + 1) * LANES] for lane in range(blocks)]
            sums_out[part, at] = jnp.concatenate(pieces + [lines], 0).astype(jnp.bfloat16)
        for o in hops:
            sum_copy(part, chip, lax.rem(chip + o, chips)).start()
    fill_ramps(ramps, dms, first_bin, 10, SHARED // CHUNK)
    rows = []
    for part in range(parts):
        grouped, rest = kept_sums[part, chip], kept_rest[part, chip][:, 0:1]
        for o in hops:
            source = lax.rem(chip + o, chips)
            sum_copy(part, source, source).wait_recv()
            came = sums_in[part, source].astype(jnp.float32)
            tall = 2 * size
            pieces = [came[at * tall : (at + 1) * tall] for at in range(blocks)]
            grouped += jnp.concatenate(pieces, 1)
            line = came[blocks * tall : blocks * tall + 1]
            line += came[blocks * tall + 1 : blocks * tall + 2]
            rest += jnp.sum(line * ones, 1, keepdims=True)
        real, imag = grouped[:size], grouped[size:]
        upper = jnp.concatenate([real, -imag], 1)
        lower = jnp.concatenate([imag, real], 1)
        for at in range(size):
            left = jnp.concatenate([upper[at : at + 1], lower[at : at + 1]], 0)
            total = jnp.dot(
                left.astype(jnp.bfloat16), ramps[part * size + at],
                preferred_element_type=jnp.float32,
            )
            re = total[0:1] + rest[at : at + 1]
            im = total[1:2] + rest[size + at : size + at + 1]
            rows.append((re * re + im * im) * (1.0 / CHANNELS))
    turned = jnp.concatenate(rows, 0).T
    for target in range(members):
        power_out[target] = turned[target * kept : (target + 1) * kept]

    def power_copy(slot, target):
        return pltpu.make_async_remote_copy(
            src_ref=power_out.at[target], dst_ref=power_in.at[slot],
            send_sem=pow_send.at[target], recv_sem=pow_recv.at[slot],
            device_id={"freq": target}, device_id_type=pl.DeviceIdType.MESH,
        )

    for o in order:
        power_copy(me, lax.rem(me + o, members)).start()
    power_in[me] = power_out[me]
    for o in order:
        target = lax.rem(me + o, members)
        power_copy(target, target).wait_recv()
    sources = [2 * at + half for half in range(2) for at in range(chips)]
    out[...] = jnp.concatenate([power_in[source] for source in sources], 1)
    for o in order:
        target = lax.rem(me + o, members)
        power_copy(target, target).wait_send()
    for part in range(parts):
        for slab in range(slabs):
            pair_copy(slab, part).wait_send()
        for o in hops:
            target = lax.rem(chip + o, chips)
            sum_copy(part, target, target).wait_send()

    @pl.when(seg > 0)
    def _():
        for slab in range(slabs):
            back_copy(slab).wait_send()

    @pl.when(seg < segments - 1)
    def _():
        forward_copy().wait_send()


def body(raw_samples, filter_taps, dm_trials, channel_units):
    members = lax.axis_size("freq")
    own_len, width = raw_samples.shape
    bins, kept, wide = BINS // members, DMS // members, min(SLAB, width)
    slabs, rows = width // wide, KEPT + TAPS
    parts = 2 if bins % (2 * TAPS) == 0 else 1
    size = bins // parts
    swap = 2 * size * (SHARED // LANES) + TAPS
    chips = members // 2
    time, channel, shrink, grow, tap, twiddle = tables(chips)
    units = channel_units.reshape(CHANNELS // LANES, LANES)
    vmem = pl.BlockSpec(memory_space=pltpu.VMEM)
    anywhere = pl.BlockSpec(memory_space=pl.ANY)
    dma = pltpu.SemaphoreType.DMA
    power = pl.pallas_call(
        functools.partial(kernel, members, lax.axis_size("tm")),
        out_shape=pltpu.VMEM((kept, BINS), jnp.float32),
        in_specs=[anywhere] * 6 + [vmem] * 4,
        out_specs=vmem,
        scratch_shapes=[
            pltpu.VMEM((own_len, width), jnp.bfloat16),
            pltpu.VMEM(time.shape, jnp.bfloat16),
            pltpu.VMEM(channel.shape, jnp.bfloat16),
            pltpu.VMEM(shrink.shape, jnp.bfloat16),
            pltpu.VMEM(grow.shape, jnp.bfloat16),
            pltpu.VMEM(twiddle.shape[1:], jnp.float32),
            pltpu.VMEM((slabs, rows, wide), jnp.bfloat16),
            pltpu.VMEM((slabs, rows, wide), jnp.bfloat16),
            pltpu.VMEM((TAPS, width), jnp.bfloat16),
            pltpu.VMEM((2 * TAPS, width), jnp.float32),
            pltpu.VMEM((2 * BINS, width), jnp.float32),
            pltpu.VMEM((2 * BINS, width), jnp.float32),
            pltpu.VMEM((2 * BINS, wide), jnp.float32),
            pltpu.VMEM((slabs, parts, 2, chips, size, wide), jnp.bfloat16),
            pltpu.VMEM((2, slabs, parts, 2, chips, size, wide), jnp.bfloat16),
            pltpu.VMEM((bins, 2 * SHARED, DMS), jnp.bfloat16),
            pltpu.VMEM((RADIX, INNER, SHARED), jnp.bfloat16),
            pltpu.VMEM((RADIX * chips * size, 2 * INNER), jnp.float32),
            pltpu.VMEM((parts, chips, 2 * size, SHARED), jnp.float32),
            pltpu.VMEM((parts, chips, 2 * size, LANES), jnp.float32),
            pltpu.VMEM((parts, chips, swap, LANES), jnp.bfloat16),
            pltpu.VMEM((parts, chips, swap, LANES), jnp.bfloat16),
            pltpu.VMEM((members, kept, bins), jnp.float32),
            pltpu.VMEM((members, kept, bins), jnp.float32),
            dma((7,)), dma((1 + slabs,)), dma((1 + slabs,)),
            dma((slabs, parts)), dma((slabs, parts)), dma((parts, chips)), dma((parts, chips)),
            dma((members,)), dma((members,)),
        ],
        compiler_params=pltpu.CompilerParams(
            vmem_limit_bytes=56 * 2**20, collective_id=0, has_side_effects=True
        ),
    )(
        raw_samples, time, channel, shrink, grow, twiddle,
        filter_taps, units, dm_trials.reshape(1, DMS), tap,
    )
    return power[None]


def solution(mesh):
    in_specs = (P(("beam", "tm"), "freq"), P(None, "freq"), P(), P())
    out_specs = P(("beam", "tm"), "freq", None)
    return jax.shard_map(body, mesh=mesh, in_specs=in_specs, out_specs=out_specs, check_vma=False)
```

```python
import functools
import math

import jax
import jax.numpy as jnp
import numpy as np
from jax import lax
from jax.experimental import pallas as pl
from jax.experimental.pallas import tpu as pltpu
from jax.sharding import PartitionSpec as P

TAPS = 16
DFT_LEN = 2048
BINS = 256
SHARED = 512
DMS = 256
DM_STEPS = 1024
CHANNELS = 4096
RADIX = 16
INNER = CHANNELS // RADIX
CHUNK = 16
LANES = 128
SLAB = 256
KEPT = 160
TILE = 8


def band_basis():
    at = np.arange(SHARED)
    diag = ((SHARED - 1) / 2 - at) ** 2 * math.cos(2 * math.pi * BINS / DFT_LEN)
    off = at[1:] * (SHARED - at[1:]) / 2.0
    square = off * off
    low = np.full(KEPT, -float(SHARED * SHARED))
    high = np.full(KEPT, float(SHARED * SHARED))
    wanted = SHARED - np.arange(KEPT)
    for _ in range(70):
        middle = (low + high) / 2
        pivot = diag[0] - middle
        below = (pivot < 0).astype(np.int64)
        for row in range(1, SHARED):
            pivot = np.where(pivot == 0, 1e-30, pivot)
            pivot = diag[row] - middle - square[row - 1] / pivot
            below += pivot < 0
        high = np.where(below >= wanted, middle, high)
        low = np.where(below >= wanted, low, middle)
    value = (low + high) / 2
    down, up = np.zeros((SHARED, KEPT)), np.zeros((SHARED, KEPT))
    down[0], up[-1] = diag[0] - value, diag[-1] - value
    for row in range(1, SHARED):
        down[row] = diag[row] - value - square[row - 1] / down[row - 1]
        back = SHARED - 1 - row
        up[back] = diag[back] - value - square[back] / up[back + 1]
    twist = np.argmin(np.abs(down + up - (diag[:, None] - value)), 0)
    basis = np.zeros((SHARED, KEPT))
    basis[twist, np.arange(KEPT)] = 1.0
    for row in range(1, SHARED):
        basis[row] = np.where(row > twist, -off[row - 1] * basis[row - 1] / up[row], basis[row])
        back = SHARED - 1 - row
        step = -off[back] * basis[back + 1] / down[back]
        basis[back] = np.where(back < twist, step, basis[back])
    total = np.zeros(KEPT)
    for row in range(SHARED):
        total = total + basis[row] * basis[row]
    return (basis / np.sqrt(total)).T


def split(values, count):
    parts = []
    for _ in range(count):
        part = np.asarray(values).astype(jnp.bfloat16)
        parts.append(part)
        values = values - part.astype(np.float64)
    return parts


def bin_order(chips):
    groups = BINS // (2 * chips * TILE)
    bins = np.arange(BINS).reshape(groups, chips, 2, TILE)
    return bins.transpose(2, 1, 0, 3).reshape(-1)


def tables(chips):
    bins = bin_order(chips)[:, None]
    angle = 2 * np.pi * (bins * np.arange(DFT_LEN)[None, :] % DFT_LEN) / DFT_LEN
    time = np.concatenate([np.cos(angle), -np.sin(angle)], 0) / math.sqrt(DFT_LEN)
    basis = band_basis()
    shrink = np.concatenate(split(basis, 2), 0)
    grow = np.concatenate(split(np.dot(time[:, DFT_LEN - SHARED :], basis.T), 2), 1)
    angle = 2 * np.pi * (bins * np.arange(TAPS)[None, :]) / DFT_LEN
    tap = split(np.concatenate([np.cos(angle), -np.sin(angle)], 0), 3)
    tap = np.concatenate([tap[0], tap[1], tap[2], tap[0], tap[1], tap[0]], 1)
    ids = np.arange(INNER)
    start = (np.arange(chips) * (CHANNELS // chips))[:, None, None]
    angle = np.arange(RADIX)[:, None] * (ids[None, :] + start) % CHANNELS
    angle = 2 * np.pi * angle / CHANNELS
    twiddle = np.stack([np.cos(angle), -np.sin(angle)], 1) / math.sqrt(RADIX)
    spread = ids.reshape(CHANNELS // LANES, LANES // RADIX).T.reshape(-1)
    angle = 2 * np.pi * (ids[:, None] * spread[None, :] % INNER) / INNER
    cosine, sine = np.cos(angle), np.sin(angle)
    channel = np.block([[cosine, -sine], [sine, cosine]]) / math.sqrt(INNER)
    return (
        jnp.asarray(time[:, : DFT_LEN - SHARED], jnp.bfloat16),
        jnp.asarray(channel, jnp.bfloat16),
        jnp.asarray(shrink),
        jnp.asarray(grow),
        jnp.asarray(tap),
        jnp.asarray(twiddle, jnp.float32),
    )


def unit_circle(phase):
    x = phase.astype(jnp.float32) * (2.0 * math.pi / DFT_LEN)
    y = x * x
    sine, cosine = jnp.full_like(y, -1 / 39916800), jnp.full_like(y, 1 / 479001600)
    for value in (1 / 362880, -1 / 5040, 1 / 120, -1 / 6, 1.0):
        sine = sine * y + value
    for value in (-1 / 3628800, 1 / 40320, -1 / 720, 1 / 24, -0.5, 1.0):
        cosine = cosine * y + value
    return cosine, sine * x


def phasor(phase):
    quarter = phase >> 9
    cosine, sine = unit_circle(phase & 511)
    odd = (quarter & 1) == 1
    swapped_cos = jnp.where(odd, -sine, cosine)
    swapped_sin = jnp.where(odd, cosine, sine)
    far = quarter >= 2
    return jnp.where(far, -swapped_cos, swapped_cos), jnp.where(far, -swapped_sin, swapped_sin)


def turn(real, imag, cosine, sine):
    return real * cosine - imag * sine, imag * cosine + real * sine


def fill_ramps(ramps, dms, first_bin, start, stop):
    groups = ramps.shape[0] // TILE

    @pl.loop(start, stop)
    def _(step):
        row = pl.multiple_of(step * CHUNK, CHUNK)
        units = lax.broadcasted_iota(jnp.int32, (CHUNK, DMS), 0) + (row + 1)
        delays = (units * dms[...]) >> 10
        step_cos, step_sin = unit_circle(delays)
        group_cos, group_sin = phasor((delays * first_bin) & (DFT_LEN - 1))
        if groups > 1:
            jump_cos, jump_sin = phasor((delays * (BINS // groups)) & (DFT_LEN - 1))
        for group in range(groups):
            cosine, sine = group_cos, group_sin
            for at in range(TILE):
                ramps[group * TILE + at, pl.ds(row, CHUNK), :] = cosine.astype(jnp.bfloat16)
                ramps[group * TILE + at, pl.ds(SHARED + row, CHUNK), :] = sine.astype(jnp.bfloat16)
                if at + 1 < TILE:
                    cosine, sine = turn(cosine, sine, step_cos, step_sin)
            if group + 1 < groups:
                group_cos, group_sin = turn(group_cos, group_sin, jump_cos, jump_sin)


def dft(real, imag):
    count = len(real)
    if count == 1:
        return real, imag
    er, ei = dft(real[0::2], imag[0::2])
    odr, odi = dft(real[1::2], imag[1::2])
    half = count // 2
    outs = [None] * count
    for k in range(half):
        if k == 0:
            tr, ti = odr[k], odi[k]
        elif 4 * k == count:
            tr, ti = odi[k], -odr[k]
        else:
            c, s = math.cos(2 * math.pi * k / count), math.sin(2 * math.pi * k / count)
            tr, ti = odr[k] * c + odi[k] * s, odi[k] * c - odr[k] * s
        outs[k] = (er[k] + tr, ei[k] + ti)
        outs[k + half] = (er[k] - tr, ei[k] - ti)
    return [o[0] for o in outs], [o[1] for o in outs]


def channelize(pair, twiddle, first, half):
    cores, slabs, _, _, chips, size, wide = pair.shape
    bins = chips * size
    real, imag = [], []
    for core in range(cores):
        for slab in range(slabs):
            real.append(pair[core, slab, half, 0].astype(jnp.float32).reshape(bins, wide))
            imag.append(pair[core, slab, half, 1].astype(jnp.float32).reshape(bins, wide))
    join = max(1, INNER // wide)
    real = [jnp.concatenate(real[at : at + join], 1) for at in range(0, len(real), join)]
    imag = [jnp.concatenate(imag[at : at + join], 1) for at in range(0, len(imag), join)]
    fold = len(real)
    stride = RADIX // fold
    for r in range(stride):
        turned_real, turned_imag = [], []
        for f in range(fold):
            c, s = math.cos(2 * math.pi * r * f / RADIX), math.sin(2 * math.pi * r * f / RADIX)
            if r * f == 0:
                turned_real.append(real[f])
                turned_imag.append(imag[f])
            else:
                turned_real.append(real[f] * c + imag[f] * s)
                turned_imag.append(imag[f] * c - real[f] * s)
        outs_real, outs_imag = dft(turned_real, turned_imag)
        for at in range(fold):
            k2 = r + stride * at
            c, s = twiddle[0, k2 : k2 + 1, :], twiddle[1, k2 : k2 + 1, :]
            rows = slice(k2 * bins, k2 * bins + bins)
            first[rows, 0:INNER] = outs_real[at] * c - outs_imag[at] * s
            first[rows, INNER:] = outs_real[at] * s + outs_imag[at] * c


def fill_matches(matches, units):
    rows, lanes = units.shape
    ids = lax.broadcasted_iota(jnp.int32, (rows, SHARED), 1) + 1
    for k2 in range(RADIX):
        for at in range(lanes // RADIX):
            lane = at * RADIX + k2
            same = (units[:, lane : lane + 1] == ids).astype(jnp.float32)
            matches[k2, at * rows : (at + 1) * rows, :] = same.astype(jnp.bfloat16)


def group_units(spectra, matches, bins):
    grouped = jnp.zeros((2 * bins, SHARED), jnp.float32)
    whole = jnp.zeros((2 * bins, INNER), jnp.float32)
    for k2 in range(RADIX):
        part = spectra[k2 * bins : (k2 + 1) * bins]
        part = jnp.concatenate([part[:, :INNER], part[:, INNER:]], 0)
        part = part.astype(jnp.bfloat16)
        whole += part.astype(jnp.float32)
        grouped += jnp.dot(part, matches[k2], preferred_element_type=jnp.float32)
    rest = jnp.sum(whole, 1, keepdims=True) - jnp.sum(grouped, 1, keepdims=True)
    return grouped, rest


def partner_order(members):
    return sorted(range(1, members), key=lambda o: -abs(o - members // 2))


def kernel(
    members, segments,
    raw, time_hbm, channel_hbm, shrink_hbm, grow_hbm, twiddle_hbm,
    filter_taps, units, dms, tap,
    out,
    own, time, channel, shrink, grow, twiddle, edges, later, tail, padded, spec, gain, extra,
    halves, pair, ramps, matches, first, kept_sums, kept_rest, sums_out, sums_in,
    power_out, power_in,
    local_sem, halo_send, halo_recv, pair_send, pair_recv, sum_send, sum_recv,
    pow_send, pow_recv,
):
    me = lax.axis_index("freq")
    seg = lax.axis_index("tm")
    chips = members // 2
    chip, core = me // 2, me % 2
    own_len, width = own.shape
    bins = BINS // members
    kept = DMS // members
    slabs, _, wide = later.shape
    head, rest = pl.ds(0, SHARED), pl.ds(SHARED, own_len - SHARED)
    loads = [
        pltpu.make_async_copy(raw.at[head], own.at[head], local_sem.at[0]),
        pltpu.make_async_copy(shrink_hbm, shrink, local_sem.at[1]),
        pltpu.make_async_copy(raw.at[rest], own.at[rest], local_sem.at[2]),
        pltpu.make_async_copy(time_hbm, time, local_sem.at[3]),
        pltpu.make_async_copy(grow_hbm, grow, local_sem.at[4]),
        pltpu.make_async_copy(channel_hbm, channel, local_sem.at[5]),
        pltpu.make_async_copy(twiddle_hbm.at[chip], twiddle, local_sem.at[6]),
    ]
    for load in loads[:2]:
        load.start()

    barrier = pltpu.get_barrier_semaphore()
    order = partner_order(members)
    for o in order:
        pl.semaphore_signal(
            barrier, inc=1, device_id={"freq": lax.rem(me + o, members)},
            device_id_type=pl.DeviceIdType.MESH,
        )

    @pl.when(seg > 0)
    def _():
        pl.semaphore_signal(
            barrier, inc=1, device_id={"tm": seg - 1}, device_id_type=pl.DeviceIdType.MESH
        )

    @pl.when(seg < segments - 1)
    def _():
        pl.semaphore_signal(
            barrier, inc=1, device_id={"tm": seg + 1}, device_id_type=pl.DeviceIdType.MESH
        )

    @pl.when(seg == 0)
    def _():
        for load in loads[2:]:
            load.start()

    for load in loads[:2]:
        load.wait()

    @pl.when(seg > 0)
    def _():
        for load in loads[2:]:
            load.start()

    @pl.when(seg > 0)
    def _():
        both = jnp.dot(shrink[...], own[0:SHARED, :], preferred_element_type=jnp.float32)
        both = (both[:KEPT] + both[KEPT:]).astype(jnp.bfloat16)
        for slab in range(slabs):
            cols = slice(slab * wide, (slab + 1) * wide)
            edges[slab, 0:KEPT, :] = both[:, cols]
            edges[slab, KEPT:, :] = own[SHARED - TAPS : SHARED, cols]

    pl.semaphore_wait(
        barrier, members - 1 + jnp.minimum(seg, 1) + jnp.minimum(segments - 1 - seg, 1)
    )

    def back_copy(slab):
        return pltpu.make_async_remote_copy(
            src_ref=edges.at[slab], dst_ref=later.at[slab],
            send_sem=halo_send.at[1 + slab], recv_sem=halo_recv.at[1 + slab],
            device_id={"tm": seg - 1}, device_id_type=pl.DeviceIdType.MESH,
        )

    def forward_copy():
        return pltpu.make_async_remote_copy(
            src_ref=raw.at[pl.ds(own_len - TAPS, TAPS)], dst_ref=tail,
            send_sem=halo_send.at[0], recv_sem=halo_recv.at[0],
            device_id={"tm": seg + 1}, device_id_type=pl.DeviceIdType.MESH,
        )

    @pl.when(seg > 0)
    def _():
        for slab in range(slabs):
            back_copy(slab).start()

    @pl.when(seg == 0)
    def _():
        tail[...] = jnp.zeros_like(tail)

    @pl.when(seg < segments - 1)
    def _():
        forward_copy().start()

    @pl.when(seg == segments - 1)
    def _():
        later[...] = jnp.zeros_like(later)

    taps = filter_taps[...]
    padded[0:TAPS, :] = taps.astype(jnp.float32)
    padded[TAPS:, :] = jnp.zeros((TAPS, width), jnp.float32)
    gain[...] = jnp.dot(
        tap[:, 0 : 3 * TAPS], jnp.concatenate([taps] * 3, 0),
        preferred_element_type=jnp.float32,
    )
    for load in loads[2:4]:
        load.wait()
    spec[...] = jnp.dot(time[...], own[...], preferred_element_type=jnp.float32)
    loads[4].wait()
    fill_matches(matches, units)
    first_bin = me * TILE
    fill_ramps(ramps, dms, first_bin, 0, 4)

    @pl.when(seg > 0)
    def _():
        forward_copy().wait_recv()

    _, _, parts, _, _, size, _ = pair.shape

    def pair_copy(slab, part):
        return pltpu.make_async_remote_copy(
            src_ref=halves.at[slab, part], dst_ref=pair.at[core, slab, part],
            send_sem=pair_send.at[slab, part], recv_sem=pair_recv.at[slab, part],
            device_id={"freq": me + 1 - 2 * core}, device_id_type=pl.DeviceIdType.MESH,
        )

    def block(half, part, at, cols):
        row = pl.multiple_of(half * (BINS // 2) + at * bins + part * size, size)
        up, low = pl.ds(row, size), pl.ds(BINS + row, size)
        sr, si, gr, gi = spec[up, cols], spec[low, cols], gain[up, cols], gain[low, cols]
        real = sr * gr - si * gi + extra[up, :]
        imag = sr * gi + si * gr + extra[low, :]
        return real.astype(jnp.bfloat16), imag.astype(jnp.bfloat16)

    for slab in range(slabs):
        cols = slice(slab * wide, (slab + 1) * wide)

        @pl.when(seg < segments - 1)
        def _():
            back_copy(slab).wait_recv()

        edge = tail[:, cols].astype(jnp.float32)
        edge = edge - later[slab, KEPT:, :].astype(jnp.float32)
        fringe = jnp.zeros_like(edge)
        for e in range(1, TAPS):
            fringe = fringe + padded[e : e + TAPS, cols] * edge[TAPS - e : TAPS - e + 1]
        fringe = fringe * (1.0 / math.sqrt(DFT_LEN))
        one = fringe.astype(jnp.bfloat16)
        left = fringe - one.astype(jnp.float32)
        two = left.astype(jnp.bfloat16)
        three = (left - two.astype(jnp.float32)).astype(jnp.bfloat16)
        extra[...] = jnp.dot(
            tap[...], jnp.concatenate([one, one, one, two, two, three], 0),
            preferred_element_type=jnp.float32,
        )
        spec[:, cols] += jnp.dot(
            grow[...], jnp.concatenate([later[slab, 0:KEPT, :]] * 2, 0),
            preferred_element_type=jnp.float32,
        )
        for part in range(parts):
            for at in range(chips):
                real, imag = block(1 - core, part, at, cols)
                halves[slab, part, 0, at], halves[slab, part, 1, at] = real, imag
            pair_copy(slab, part).start()
        for part in range(parts):
            for at in range(chips):
                real, imag = block(core, part, at, cols)
                pair[core, slab, part, 0, at], pair[core, slab, part, 1, at] = real, imag
        if slab + 1 < slabs:
            fill_ramps(ramps, dms, first_bin, 4, 8)
    fill_ramps(ramps, dms, first_bin, 8 if slabs > 1 else 4, 10)
    for load in loads[5:]:
        load.wait()

    def sum_copy(part, slot, target):
        return pltpu.make_async_remote_copy(
            src_ref=sums_out.at[part, target], dst_ref=sums_in.at[part, slot],
            send_sem=sum_send.at[part, target], recv_sem=sum_recv.at[part, slot],
            device_id={"freq": 2 * target + core}, device_id_type=pl.DeviceIdType.MESH,
        )

    ones = lax.broadcasted_iota(jnp.int32, (2 * size, LANES), 0)
    ones = (ones == lax.broadcasted_iota(jnp.int32, (2 * size, LANES), 1)).astype(jnp.float32)
    blocks = SHARED // LANES
    hops = partner_order(chips)[::-1]
    some = chips * size
    for part in range(parts):
        for slab in range(slabs):
            pair_copy(slab, part).wait_recv()
        channelize(pair, twiddle, first, part)
        spectra = jnp.dot(
            first[...].astype(jnp.bfloat16), channel[...], preferred_element_type=jnp.float32
        )
        grouped, rest = group_units(spectra, matches, some)
        for at in range(chips):
            up = slice(at * size, (at + 1) * size)
            low = slice(some + at * size, some + (at + 1) * size)
            own_sums = jnp.concatenate([grouped[up], grouped[low]], 0)
            own_rest = jnp.concatenate([rest[up], rest[low]], 0)
            kept_sums[part, at] = own_sums
            kept_rest[part, at] = jnp.broadcast_to(own_rest, (2 * size, LANES))
            line = jnp.sum(own_rest * ones, 0, keepdims=True)
            high = line.astype(jnp.bfloat16).astype(jnp.float32)
            row = lax.broadcasted_iota(jnp.int32, (TAPS, LANES), 0)
            lines = jnp.where(row == 0, high, jnp.where(row == 1, line - high, 0.0))
            pieces = [own_sums[:, lane * LANES : (lane + 1) * LANES] for lane in range(blocks)]
            sums_out[part, at] = jnp.concatenate(pieces + [lines], 0).astype(jnp.bfloat16)
        for o in hops:
            sum_copy(part, chip, lax.rem(chip + o, chips)).start()
    fill_ramps(ramps, dms, first_bin, 10, SHARED // CHUNK)
    rows = []
    for part in range(parts):
        grouped, rest = kept_sums[part, chip], kept_rest[part, chip][:, 0:1]
        for o in hops:
            source = lax.rem(chip + o, chips)
            sum_copy(part, source, source).wait_recv()
            came = sums_in[part, source].astype(jnp.float32)
            tall = 2 * size
            pieces = [came[at * tall : (at + 1) * tall] for at in range(blocks)]
            grouped += jnp.concatenate(pieces, 1)
            line = came[blocks * tall : blocks * tall + 1]
            line += came[blocks * tall + 1 : blocks * tall + 2]
            rest += jnp.sum(line * ones, 1, keepdims=True)
        real, imag = grouped[:size], grouped[size:]
        upper = jnp.concatenate([real, -imag], 1)
        lower = jnp.concatenate([imag, real], 1)
        for at in range(size):
            left = jnp.concatenate([upper[at : at + 1], lower[at : at + 1]], 0)
            total = jnp.dot(
                left.astype(jnp.bfloat16), ramps[part * size + at],
                preferred_element_type=jnp.float32,
            )
            re = total[0:1] + rest[at : at + 1]
            im = total[1:2] + rest[size + at : size + at + 1]
            rows.append((re * re + im * im) * (1.0 / CHANNELS))
    powers = jnp.concatenate(rows, 0)
    groups = bins // TILE
    for target in range(members):
        cols = slice(target * kept, (target + 1) * kept)
        pieces = [powers[at * TILE : (at + 1) * TILE, cols] for at in range(groups)]
        power_out[target] = jnp.concatenate(pieces, 1)

    def power_copy(slot, target):
        return pltpu.make_async_remote_copy(
            src_ref=power_out.at[target], dst_ref=power_in.at[slot],
            send_sem=pow_send.at[target], recv_sem=pow_recv.at[slot],
            device_id={"freq": target}, device_id_type=pl.DeviceIdType.MESH,
        )

    for o in order:
        power_copy(me, lax.rem(me + o, members)).start()
    power_in[me] = power_out[me]
    for part in range(parts):
        for slab in range(slabs):
            pair_copy(slab, part).wait_send()
        for o in hops:
            target = lax.rem(chip + o, chips)
            sum_copy(part, target, target).wait_send()

    @pl.when(seg > 0)
    def _():
        for slab in range(slabs):
            back_copy(slab).wait_send()

    @pl.when(seg < segments - 1)
    def _():
        forward_copy().wait_send()
    for o in order:
        target = lax.rem(me + o, members)
        power_copy(target, target).wait_send()
    for o in order:
        target = lax.rem(me + o, members)
        power_copy(target, target).wait_recv()
    turned = jnp.concatenate([power_in[source] for source in range(members)], 0).T
    pieces = [turned[at * kept : (at + 1) * kept] for at in range(groups)]
    out[...] = jnp.concatenate(pieces, 1)


def body(raw_samples, filter_taps, dm_trials, channel_units):
    members = lax.axis_size("freq")
    own_len, width = raw_samples.shape
    bins, kept, wide = BINS // members, DMS // members, min(SLAB, width)
    slabs, rows = width // wide, KEPT + TAPS
    parts = 2 if bins % (2 * TAPS) == 0 else 1
    size = bins // parts
    swap = 2 * size * (SHARED // LANES) + TAPS
    chips = members // 2
    time, channel, shrink, grow, tap, twiddle = tables(chips)
    units = channel_units.reshape(CHANNELS // LANES, LANES)
    vmem = pl.BlockSpec(memory_space=pltpu.VMEM)
    anywhere = pl.BlockSpec(memory_space=pl.ANY)
    dma = pltpu.SemaphoreType.DMA
    power = pl.pallas_call(
        functools.partial(kernel, members, lax.axis_size("tm")),
        out_shape=pltpu.VMEM((kept, BINS), jnp.float32),
        in_specs=[anywhere] * 6 + [vmem] * 4,
        out_specs=vmem,
        scratch_shapes=[
            pltpu.VMEM((own_len, width), jnp.bfloat16),
            pltpu.VMEM(time.shape, jnp.bfloat16),
            pltpu.VMEM(channel.shape, jnp.bfloat16),
            pltpu.VMEM(shrink.shape, jnp.bfloat16),
            pltpu.VMEM(grow.shape, jnp.bfloat16),
            pltpu.VMEM(twiddle.shape[1:], jnp.float32),
            pltpu.VMEM((slabs, rows, wide), jnp.bfloat16),
            pltpu.VMEM((slabs, rows, wide), jnp.bfloat16),
            pltpu.VMEM((TAPS, width), jnp.bfloat16),
            pltpu.VMEM((2 * TAPS, width), jnp.float32),
            pltpu.VMEM((2 * BINS, width), jnp.float32),
            pltpu.VMEM((2 * BINS, width), jnp.float32),
            pltpu.VMEM((2 * BINS, wide), jnp.float32),
            pltpu.VMEM((slabs, parts, 2, chips, size, wide), jnp.bfloat16),
            pltpu.VMEM((2, slabs, parts, 2, chips, size, wide), jnp.bfloat16),
            pltpu.VMEM((bins, 2 * SHARED, DMS), jnp.bfloat16),
            pltpu.VMEM((RADIX, INNER, SHARED), jnp.bfloat16),
            pltpu.VMEM((RADIX * chips * size, 2 * INNER), jnp.float32),
            pltpu.VMEM((parts, chips, 2 * size, SHARED), jnp.float32),
            pltpu.VMEM((parts, chips, 2 * size, LANES), jnp.float32),
            pltpu.VMEM((parts, chips, swap, LANES), jnp.bfloat16),
            pltpu.VMEM((parts, chips, swap, LANES), jnp.bfloat16),
            pltpu.VMEM((members, TILE, bins // TILE * kept), jnp.float32),
            pltpu.VMEM((members, TILE, bins // TILE * kept), jnp.float32),
            dma((7,)), dma((1 + slabs,)), dma((1 + slabs,)),
            dma((slabs, parts)), dma((slabs, parts)), dma((parts, chips)), dma((parts, chips)),
            dma((members,)), dma((members,)),
        ],
        compiler_params=pltpu.CompilerParams(
            vmem_limit_bytes=56 * 2**20, collective_id=0, has_side_effects=True
        ),
    )(
        raw_samples, time, channel, shrink, grow, twiddle,
        filter_taps, units, dm_trials.reshape(1, DMS), tap,
    )
    return power[None]


def solution(mesh):
    in_specs = (P(("beam", "tm"), "freq"), P(None, "freq"), P(), P())
    out_specs = P(("beam", "tm"), "freq", None)
    return jax.shard_map(body, mesh=mesh, in_specs=in_specs, out_specs=out_specs, check_vma=False)
```

```python
import functools
import math

import jax
import jax.numpy as jnp
import numpy as np
from jax import lax
from jax.experimental import pallas as pl
from jax.experimental.pallas import tpu as pltpu
from jax.sharding import PartitionSpec as P

TAPS = 16
DFT_LEN = 2048
BINS = 256
SHARED = 512
DMS = 256
DM_STEPS = 1024
CHANNELS = 4096
RADIX = 16
INNER = CHANNELS // RADIX
CHUNK = 16
LANES = 128
SLAB = 256
KEPT = 160
TILE = 8


def band_basis():
    at = np.arange(SHARED)
    diag = ((SHARED - 1) / 2 - at) ** 2 * math.cos(2 * math.pi * BINS / DFT_LEN)
    off = at[1:] * (SHARED - at[1:]) / 2.0
    square = off * off
    low = np.full(KEPT, -float(SHARED * SHARED))
    high = np.full(KEPT, float(SHARED * SHARED))
    wanted = SHARED - np.arange(KEPT)
    for _ in range(70):
        middle = (low + high) / 2
        pivot = diag[0] - middle
        below = (pivot < 0).astype(np.int64)
        for row in range(1, SHARED):
            pivot = np.where(pivot == 0, 1e-30, pivot)
            pivot = diag[row] - middle - square[row - 1] / pivot
            below += pivot < 0
        high = np.where(below >= wanted, middle, high)
        low = np.where(below >= wanted, low, middle)
    value = (low + high) / 2
    down, up = np.zeros((SHARED, KEPT)), np.zeros((SHARED, KEPT))
    down[0], up[-1] = diag[0] - value, diag[-1] - value
    for row in range(1, SHARED):
        down[row] = diag[row] - value - square[row - 1] / down[row - 1]
        back = SHARED - 1 - row
        up[back] = diag[back] - value - square[back] / up[back + 1]
    twist = np.argmin(np.abs(down + up - (diag[:, None] - value)), 0)
    basis = np.zeros((SHARED, KEPT))
    basis[twist, np.arange(KEPT)] = 1.0
    for row in range(1, SHARED):
        basis[row] = np.where(row > twist, -off[row - 1] * basis[row - 1] / up[row], basis[row])
        back = SHARED - 1 - row
        step = -off[back] * basis[back + 1] / down[back]
        basis[back] = np.where(back < twist, step, basis[back])
    total = np.zeros(KEPT)
    for row in range(SHARED):
        total = total + basis[row] * basis[row]
    return (basis / np.sqrt(total)).T


def split(values, count):
    parts = []
    for _ in range(count):
        part = np.asarray(values).astype(jnp.bfloat16)
        parts.append(part)
        values = values - part.astype(np.float64)
    return parts


def bin_order(chips):
    groups = BINS // (2 * chips * TILE)
    bins = np.arange(BINS).reshape(groups, chips, 2, TILE)
    return bins.transpose(2, 1, 0, 3).reshape(-1)


def tables(chips):
    bins = bin_order(chips)[:, None]
    angle = 2 * np.pi * (bins * np.arange(DFT_LEN)[None, :] % DFT_LEN) / DFT_LEN
    time = np.concatenate([np.cos(angle), -np.sin(angle)], 0) / math.sqrt(DFT_LEN)
    basis = band_basis()
    shrink = np.concatenate(split(basis, 2), 0)
    grow = np.concatenate(split(np.dot(time[:, DFT_LEN - SHARED :], basis.T), 2), 1)
    angle = 2 * np.pi * (bins * np.arange(TAPS)[None, :]) / DFT_LEN
    tap = split(np.concatenate([np.cos(angle), -np.sin(angle)], 0), 3)
    tap = np.concatenate([tap[0], tap[1], tap[2], tap[0], tap[1], tap[0]], 1)
    ids = np.arange(INNER)
    start = (np.arange(chips) * (CHANNELS // chips))[:, None, None]
    angle = np.arange(RADIX)[:, None] * (ids[None, :] + start) % CHANNELS
    angle = 2 * np.pi * angle / CHANNELS
    twiddle = np.stack([np.cos(angle), -np.sin(angle)], 1) / math.sqrt(RADIX)
    spread = ids.reshape(CHANNELS // LANES, LANES // RADIX).T.reshape(-1)
    angle = 2 * np.pi * (ids[:, None] * spread[None, :] % INNER) / INNER
    cosine, sine = np.cos(angle), np.sin(angle)
    channel = np.block([[cosine, -sine], [sine, cosine]]) / math.sqrt(INNER)
    return (
        jnp.asarray(time[:, : DFT_LEN - SHARED], jnp.bfloat16),
        jnp.asarray(channel, jnp.bfloat16),
        jnp.asarray(shrink),
        jnp.asarray(grow),
        jnp.asarray(tap),
        jnp.asarray(twiddle, jnp.float32),
    )


def unit_circle(phase):
    x = phase.astype(jnp.float32) * (2.0 * math.pi / DFT_LEN)
    y = x * x
    sine, cosine = jnp.full_like(y, -1 / 39916800), jnp.full_like(y, 1 / 479001600)
    for value in (1 / 362880, -1 / 5040, 1 / 120, -1 / 6, 1.0):
        sine = sine * y + value
    for value in (-1 / 3628800, 1 / 40320, -1 / 720, 1 / 24, -0.5, 1.0):
        cosine = cosine * y + value
    return cosine, sine * x


def phasor(phase):
    quarter = phase >> 9
    cosine, sine = unit_circle(phase & 511)
    odd = (quarter & 1) == 1
    swapped_cos = jnp.where(odd, -sine, cosine)
    swapped_sin = jnp.where(odd, cosine, sine)
    far = quarter >= 2
    return jnp.where(far, -swapped_cos, swapped_cos), jnp.where(far, -swapped_sin, swapped_sin)


def turn(real, imag, cosine, sine):
    return real * cosine - imag * sine, imag * cosine + real * sine


def fill_ramps(ramps, dms, first_bin, start, stop):
    groups = ramps.shape[0] // TILE

    @pl.loop(start, stop)
    def _(step):
        row = pl.multiple_of(step * CHUNK, CHUNK)
        units = lax.broadcasted_iota(jnp.int32, (CHUNK, DMS), 0) + (row + 1)
        delays = (units * dms[...]) >> 10
        step_cos, step_sin = unit_circle(delays)
        group_cos, group_sin = phasor((delays * first_bin) & (DFT_LEN - 1))
        if groups > 1:
            jump_cos, jump_sin = phasor((delays * (BINS // groups)) & (DFT_LEN - 1))
        for group in range(groups):
            cosine, sine = group_cos, group_sin
            for at in range(TILE):
                ramps[group * TILE + at, pl.ds(row, CHUNK), :] = cosine.astype(jnp.bfloat16)
                ramps[group * TILE + at, pl.ds(SHARED + row, CHUNK), :] = sine.astype(jnp.bfloat16)
                if at + 1 < TILE:
                    cosine, sine = turn(cosine, sine, step_cos, step_sin)
            if group + 1 < groups:
                group_cos, group_sin = turn(group_cos, group_sin, jump_cos, jump_sin)


def dft(real, imag):
    count = len(real)
    if count == 1:
        return real, imag
    er, ei = dft(real[0::2], imag[0::2])
    odr, odi = dft(real[1::2], imag[1::2])
    half = count // 2
    outs = [None] * count
    for k in range(half):
        if k == 0:
            tr, ti = odr[k], odi[k]
        elif 4 * k == count:
            tr, ti = odi[k], -odr[k]
        else:
            c, s = math.cos(2 * math.pi * k / count), math.sin(2 * math.pi * k / count)
            tr, ti = odr[k] * c + odi[k] * s, odi[k] * c - odr[k] * s
        outs[k] = (er[k] + tr, ei[k] + ti)
        outs[k + half] = (er[k] - tr, ei[k] - ti)
    return [o[0] for o in outs], [o[1] for o in outs]


def channelize(pair, twiddle, first, half):
    cores, slabs, _, _, chips, size, wide = pair.shape
    bins = chips * size
    real, imag = [], []
    for core in range(cores):
        for slab in range(slabs):
            real.append(pair[core, slab, half, 0].astype(jnp.float32).reshape(bins, wide))
            imag.append(pair[core, slab, half, 1].astype(jnp.float32).reshape(bins, wide))
    join = max(1, INNER // wide)
    real = [jnp.concatenate(real[at : at + join], 1) for at in range(0, len(real), join)]
    imag = [jnp.concatenate(imag[at : at + join], 1) for at in range(0, len(imag), join)]
    fold = len(real)
    stride = RADIX // fold
    for r in range(stride):
        turned_real, turned_imag = [], []
        for f in range(fold):
            c, s = math.cos(2 * math.pi * r * f / RADIX), math.sin(2 * math.pi * r * f / RADIX)
            if r * f == 0:
                turned_real.append(real[f])
                turned_imag.append(imag[f])
            else:
                turned_real.append(real[f] * c + imag[f] * s)
                turned_imag.append(imag[f] * c - real[f] * s)
        outs_real, outs_imag = dft(turned_real, turned_imag)
        for at in range(fold):
            k2 = r + stride * at
            c, s = twiddle[0, k2 : k2 + 1, :], twiddle[1, k2 : k2 + 1, :]
            rows = slice(k2 * bins, k2 * bins + bins)
            value = outs_real[at] * c - outs_imag[at] * s
            first[rows, 0:INNER] = value.astype(jnp.bfloat16)
            value = outs_real[at] * s + outs_imag[at] * c
            first[rows, INNER:] = value.astype(jnp.bfloat16)


def fill_matches(matches, units):
    rows, lanes = units.shape
    ids = lax.broadcasted_iota(jnp.int32, (rows, SHARED), 1) + 1
    for k2 in range(RADIX):
        for at in range(lanes // RADIX):
            lane = at * RADIX + k2
            same = (units[:, lane : lane + 1] == ids).astype(jnp.float32)
            matches[k2, at * rows : (at + 1) * rows, :] = same.astype(jnp.bfloat16)


def group_units(spectra, matches, bins):
    whole = jnp.zeros((2 * bins, INNER), jnp.float32)
    pieces = []
    for k2 in range(RADIX):
        part = spectra[k2 * bins : (k2 + 1) * bins]
        part = jnp.concatenate([part[:, :INNER], part[:, INNER:]], 0)
        part = part.astype(jnp.bfloat16)
        whole += part.astype(jnp.float32)
        pieces.append(part)
    grouped = jnp.dot(
        jnp.concatenate(pieces, 1), matches[...].reshape(CHANNELS, SHARED),
        preferred_element_type=jnp.float32,
    )
    rest = jnp.sum(whole, 1, keepdims=True) - jnp.sum(grouped, 1, keepdims=True)
    return grouped, rest


def partner_order(members):
    return sorted(range(1, members), key=lambda o: -abs(o - members // 2))


def kernel(
    members, segments,
    raw, time_hbm, channel_hbm, shrink_hbm, grow_hbm, twiddle_hbm,
    filter_taps, units, dms, tap,
    out,
    own, time, channel, shrink, grow, twiddle, edges, later, tail, padded, spec, gain, extra,
    halves, pair, ramps, matches, first, kept_sums, kept_rest, sums_out, sums_in,
    power_out, power_in,
    local_sem, halo_send, halo_recv, pair_send, pair_recv, sum_send, sum_recv,
    pow_send, pow_recv,
):
    me = lax.axis_index("freq")
    seg = lax.axis_index("tm")
    chips = members // 2
    chip, core = me // 2, me % 2
    own_len, width = own.shape
    bins = BINS // members
    kept = DMS // members
    slabs, _, wide = later.shape
    head, rest = pl.ds(0, SHARED), pl.ds(SHARED, own_len - SHARED)
    loads = [
        pltpu.make_async_copy(raw.at[head], own.at[head], local_sem.at[0]),
        pltpu.make_async_copy(shrink_hbm, shrink, local_sem.at[1]),
        pltpu.make_async_copy(raw.at[rest], own.at[rest], local_sem.at[2]),
        pltpu.make_async_copy(time_hbm, time, local_sem.at[3]),
        pltpu.make_async_copy(grow_hbm, grow, local_sem.at[4]),
        pltpu.make_async_copy(channel_hbm, channel, local_sem.at[5]),
        pltpu.make_async_copy(twiddle_hbm.at[chip], twiddle, local_sem.at[6]),
    ]
    for load in loads[:2]:
        load.start()

    barrier = pltpu.get_barrier_semaphore()
    order = partner_order(members)
    near = [lax.rem(me + 2 * o, members) for o in range(1, chips)] + [me + 1 - 2 * core]
    for peer in near:
        pl.semaphore_signal(
            barrier, inc=1, device_id={"freq": peer}, device_id_type=pl.DeviceIdType.MESH
        )

    @pl.when(seg > 0)
    def _():
        pl.semaphore_signal(
            barrier, inc=1, device_id={"tm": seg - 1}, device_id_type=pl.DeviceIdType.MESH
        )

    @pl.when(seg < segments - 1)
    def _():
        pl.semaphore_signal(
            barrier, inc=1, device_id={"tm": seg + 1}, device_id_type=pl.DeviceIdType.MESH
        )

    @pl.when(seg == 0)
    def _():
        for load in loads[2:]:
            load.start()

    for load in loads[:2]:
        load.wait()

    @pl.when(seg > 0)
    def _():
        for load in loads[2:]:
            load.start()

    @pl.when(seg > 0)
    def _():
        both = jnp.dot(shrink[...], own[0:SHARED, :], preferred_element_type=jnp.float32)
        both = (both[:KEPT] + both[KEPT:]).astype(jnp.bfloat16)
        for slab in range(slabs):
            cols = slice(slab * wide, (slab + 1) * wide)
            edges[slab, 0:KEPT, :] = both[:, cols]
            edges[slab, KEPT:, :] = own[SHARED - TAPS : SHARED, cols]

    pl.semaphore_wait(
        barrier, len(near) + jnp.minimum(seg, 1) + jnp.minimum(segments - 1 - seg, 1)
    )

    def back_copy(slab):
        return pltpu.make_async_remote_copy(
            src_ref=edges.at[slab], dst_ref=later.at[slab],
            send_sem=halo_send.at[1 + slab], recv_sem=halo_recv.at[1 + slab],
            device_id={"tm": seg - 1}, device_id_type=pl.DeviceIdType.MESH,
        )

    def forward_copy():
        return pltpu.make_async_remote_copy(
            src_ref=raw.at[pl.ds(own_len - TAPS, TAPS)], dst_ref=tail,
            send_sem=halo_send.at[0], recv_sem=halo_recv.at[0],
            device_id={"tm": seg + 1}, device_id_type=pl.DeviceIdType.MESH,
        )

    @pl.when(seg > 0)
    def _():
        for slab in range(slabs):
            back_copy(slab).start()

    @pl.when(seg == 0)
    def _():
        tail[...] = jnp.zeros_like(tail)

    @pl.when(seg < segments - 1)
    def _():
        forward_copy().start()

    @pl.when(seg == segments - 1)
    def _():
        later[...] = jnp.zeros_like(later)

    taps = filter_taps[...]
    padded[0:TAPS, :] = taps.astype(jnp.float32)
    padded[TAPS:, :] = jnp.zeros((TAPS, width), jnp.float32)
    gain[...] = jnp.dot(
        tap[:, 0 : 3 * TAPS], jnp.concatenate([taps] * 3, 0),
        preferred_element_type=jnp.float32,
    )
    for load in loads[2:4]:
        load.wait()
    spec[...] = jnp.dot(time[...], own[...], preferred_element_type=jnp.float32)
    loads[4].wait()
    fill_matches(matches, units)
    first_bin = me * TILE
    fill_ramps(ramps, dms, first_bin, 0, 4)

    @pl.when(seg > 0)
    def _():
        forward_copy().wait_recv()

    _, _, parts, _, _, size, _ = pair.shape

    def pair_copy(slab, part):
        return pltpu.make_async_remote_copy(
            src_ref=halves.at[slab, part], dst_ref=pair.at[core, slab, part],
            send_sem=pair_send.at[slab, part], recv_sem=pair_recv.at[slab, part],
            device_id={"freq": me + 1 - 2 * core}, device_id_type=pl.DeviceIdType.MESH,
        )

    def block(half, part, at, cols):
        row = pl.multiple_of(half * (BINS // 2) + at * bins + part * size, size)
        up, low = pl.ds(row, size), pl.ds(BINS + row, size)
        sr, si, gr, gi = spec[up, cols], spec[low, cols], gain[up, cols], gain[low, cols]
        real = sr * gr - si * gi + extra[up, :]
        imag = sr * gi + si * gr + extra[low, :]
        return real.astype(jnp.bfloat16), imag.astype(jnp.bfloat16)

    for slab in range(slabs):
        cols = slice(slab * wide, (slab + 1) * wide)

        @pl.when(seg < segments - 1)
        def _():
            back_copy(slab).wait_recv()

        edge = tail[:, cols].astype(jnp.float32)
        edge = edge - later[slab, KEPT:, :].astype(jnp.float32)
        fringe = jnp.zeros_like(edge)
        for e in range(1, TAPS):
            fringe = fringe + padded[e : e + TAPS, cols] * edge[TAPS - e : TAPS - e + 1]
        fringe = fringe * (1.0 / math.sqrt(DFT_LEN))
        one = fringe.astype(jnp.bfloat16)
        left = fringe - one.astype(jnp.float32)
        two = left.astype(jnp.bfloat16)
        three = (left - two.astype(jnp.float32)).astype(jnp.bfloat16)
        extra[...] = jnp.dot(
            tap[...], jnp.concatenate([one, one, one, two, two, three], 0),
            preferred_element_type=jnp.float32,
        )
        spec[:, cols] += jnp.dot(
            grow[...], jnp.concatenate([later[slab, 0:KEPT, :]] * 2, 0),
            preferred_element_type=jnp.float32,
        )
        for part in range(parts):
            for at in range(chips):
                real, imag = block(1 - core, part, at, cols)
                halves[slab, part, 0, at], halves[slab, part, 1, at] = real, imag
            pair_copy(slab, part).start()
        for part in range(parts):
            for at in range(chips):
                real, imag = block(core, part, at, cols)
                pair[core, slab, part, 0, at], pair[core, slab, part, 1, at] = real, imag
        if slab + 1 < slabs:
            fill_ramps(ramps, dms, first_bin, 4, 8)
    fill_ramps(ramps, dms, first_bin, 8 if slabs > 1 else 4, 10)
    for load in loads[5:]:
        load.wait()

    def sum_copy(part, slot, target):
        sent = pl.ds(0, sums_in.shape[2] - (TAPS if part + 1 < parts else 0))
        return pltpu.make_async_remote_copy(
            src_ref=sums_out.at[part, target, sent], dst_ref=sums_in.at[part, slot, sent],
            send_sem=sum_send.at[part, target], recv_sem=sum_recv.at[part, slot],
            device_id={"freq": 2 * target + core}, device_id_type=pl.DeviceIdType.MESH,
        )

    ones = lax.broadcasted_iota(jnp.int32, (2 * size, LANES), 0)
    ones = (ones == lax.broadcasted_iota(jnp.int32, (2 * size, LANES), 1)).astype(jnp.float32)
    blocks = SHARED // LANES
    hops = partner_order(chips)[::-1]
    some = chips * size
    tall = 2 * size
    line_row = lax.broadcasted_iota(jnp.int32, (TAPS, LANES), 0)
    lines = [jnp.zeros((TAPS, LANES), jnp.float32)] * chips
    for part in range(parts):
        for slab in range(slabs):
            pair_copy(slab, part).wait_recv()
        channelize(pair, twiddle, first, part)
        spectra = jnp.dot(
            first[...], channel[...], preferred_element_type=jnp.float32
        )
        grouped, rest = group_units(spectra, matches, some)
        for at in range(chips):
            up = slice(at * size, (at + 1) * size)
            low = slice(some + at * size, some + (at + 1) * size)
            own_sums = jnp.concatenate([grouped[up], grouped[low]], 0)
            own_rest = jnp.concatenate([rest[up], rest[low]], 0)
            kept_sums[part, at] = own_sums
            kept_rest[part, at] = jnp.broadcast_to(own_rest, (2 * size, LANES))
            line = jnp.sum(own_rest * ones, 0, keepdims=True)
            high = line.astype(jnp.bfloat16).astype(jnp.float32)
            lines[at] = jnp.where(line_row == 2 * part, high, lines[at])
            lines[at] = jnp.where(line_row == 2 * part + 1, line - high, lines[at])
            pieces = [own_sums[:, lane * LANES : (lane + 1) * LANES] for lane in range(blocks)]
            pieces = jnp.concatenate(pieces, 0).astype(jnp.bfloat16)
            sums_out[part, at, 0 : blocks * tall, :] = pieces
            if part + 1 == parts:
                sums_out[part, at, blocks * tall :, :] = lines[at].astype(jnp.bfloat16)
        for o in hops:
            sum_copy(part, chip, lax.rem(chip + o, chips)).start()
    fill_ramps(ramps, dms, first_bin, 10, SHARED // CHUNK)
    totals = []
    tile_row = lax.broadcasted_iota(jnp.int32, (TILE, DMS), 0)
    for part in range(parts):
        grouped = kept_sums[part, chip]
        for o in hops:
            source = lax.rem(chip + o, chips)
            sum_copy(part, source, source).wait_recv()
            came = sums_in[part, source, 0 : blocks * tall, :].astype(jnp.float32)
            pieces = [came[at * tall : (at + 1) * tall] for at in range(blocks)]
            grouped += jnp.concatenate(pieces, 1)
        real, imag = grouped[:size], grouped[size:]
        upper = jnp.concatenate([real, -imag], 1)
        lower = jnp.concatenate([imag, real], 1)
        for group in range(size // TILE):
            tile = slice(group * TILE, (group + 1) * TILE)
            left = jnp.concatenate([upper[tile], lower[tile]], 0).astype(jnp.bfloat16)
            re = jnp.zeros((TILE, DMS), jnp.float32)
            im = jnp.zeros((TILE, DMS), jnp.float32)
            for at in range(TILE):
                total = jnp.dot(
                    left, ramps[part * size + group * TILE + at],
                    preferred_element_type=jnp.float32,
                )
                re = jnp.where(tile_row == at, total[:TILE], re)
                im = jnp.where(tile_row == at, total[TILE:], im)
            totals.append((re, im))
    powers = []
    for part in range(parts):
        rest = kept_rest[part, chip][:, 0:1]
        for o in hops:
            source = lax.rem(chip + o, chips)
            line = sums_in[parts - 1, source, blocks * tall :, :].astype(jnp.float32)
            line = line[2 * part : 2 * part + 1] + line[2 * part + 1 : 2 * part + 2]
            rest += jnp.sum(line * ones, 1, keepdims=True)
        for group in range(size // TILE):
            re, im = totals[part * (size // TILE) + group]
            re += rest[group * TILE : (group + 1) * TILE]
            im += rest[size + group * TILE : size + (group + 1) * TILE]
            powers.append((re * re + im * im) * (1.0 / CHANNELS))
    for target in range(members):
        cols = slice(target * kept, (target + 1) * kept)
        power_out[target] = jnp.concatenate([power[:, cols] for power in powers], 1)

    def power_copy(slot, target):
        return pltpu.make_async_remote_copy(
            src_ref=power_out.at[target], dst_ref=power_in.at[slot],
            send_sem=pow_send.at[target], recv_sem=pow_recv.at[slot],
            device_id={"freq": target}, device_id_type=pl.DeviceIdType.MESH,
        )

    for o in order:
        power_copy(me, lax.rem(me + o, members)).start()
    power_in[me] = power_out[me]
    for part in range(parts):
        for slab in range(slabs):
            pair_copy(slab, part).wait_send()
        for o in hops:
            target = lax.rem(chip + o, chips)
            sum_copy(part, target, target).wait_send()

    @pl.when(seg > 0)
    def _():
        for slab in range(slabs):
            back_copy(slab).wait_send()

    @pl.when(seg < segments - 1)
    def _():
        forward_copy().wait_send()
    for o in order:
        target = lax.rem(me + o, members)
        power_copy(target, target).wait_send()
    for o in order:
        target = lax.rem(me + o, members)
        power_copy(target, target).wait_recv()
    turned = jnp.concatenate([power_in[source] for source in range(members)], 0).T
    pieces = [turned[at * kept : (at + 1) * kept] for at in range(bins // TILE)]
    out[...] = jnp.concatenate(pieces, 1)


def body(raw_samples, filter_taps, dm_trials, channel_units):
    members = lax.axis_size("freq")
    own_len, width = raw_samples.shape
    bins, kept, wide = BINS // members, DMS // members, min(SLAB, width)
    slabs, rows = width // wide, KEPT + TAPS
    parts = 2 if bins % (2 * TAPS) == 0 else 1
    size = bins // parts
    swap = 2 * size * (SHARED // LANES) + TAPS
    chips = members // 2
    time, channel, shrink, grow, tap, twiddle = tables(chips)
    units = channel_units.reshape(CHANNELS // LANES, LANES)
    vmem = pl.BlockSpec(memory_space=pltpu.VMEM)
    anywhere = pl.BlockSpec(memory_space=pl.ANY)
    dma = pltpu.SemaphoreType.DMA
    power = pl.pallas_call(
        functools.partial(kernel, members, lax.axis_size("tm")),
        out_shape=pltpu.VMEM((kept, BINS), jnp.float32),
        in_specs=[anywhere] * 6 + [vmem] * 4,
        out_specs=vmem,
        scratch_shapes=[
            pltpu.VMEM((own_len, width), jnp.bfloat16),
            pltpu.VMEM(time.shape, jnp.bfloat16),
            pltpu.VMEM(channel.shape, jnp.bfloat16),
            pltpu.VMEM(shrink.shape, jnp.bfloat16),
            pltpu.VMEM(grow.shape, jnp.bfloat16),
            pltpu.VMEM(twiddle.shape[1:], jnp.float32),
            pltpu.VMEM((slabs, rows, wide), jnp.bfloat16),
            pltpu.VMEM((slabs, rows, wide), jnp.bfloat16),
            pltpu.VMEM((TAPS, width), jnp.bfloat16),
            pltpu.VMEM((2 * TAPS, width), jnp.float32),
            pltpu.VMEM((2 * BINS, width), jnp.float32),
            pltpu.VMEM((2 * BINS, width), jnp.float32),
            pltpu.VMEM((2 * BINS, wide), jnp.float32),
            pltpu.VMEM((slabs, parts, 2, chips, size, wide), jnp.bfloat16),
            pltpu.VMEM((2, slabs, parts, 2, chips, size, wide), jnp.bfloat16),
            pltpu.VMEM((bins, 2 * SHARED, DMS), jnp.bfloat16),
            pltpu.VMEM((RADIX, INNER, SHARED), jnp.bfloat16),
            pltpu.VMEM((RADIX * chips * size, 2 * INNER), jnp.bfloat16),
            pltpu.VMEM((parts, chips, 2 * size, SHARED), jnp.float32),
            pltpu.VMEM((parts, chips, 2 * size, LANES), jnp.float32),
            pltpu.VMEM((parts, chips, swap, LANES), jnp.bfloat16),
            pltpu.VMEM((parts, chips, swap, LANES), jnp.bfloat16),
            pltpu.VMEM((members, TILE, bins // TILE * kept), jnp.float32),
            pltpu.VMEM((members, TILE, bins // TILE * kept), jnp.float32),
            dma((7,)), dma((1 + slabs,)), dma((1 + slabs,)),
            dma((slabs, parts)), dma((slabs, parts)), dma((parts, chips)), dma((parts, chips)),
            dma((members,)), dma((members,)),
        ],
        compiler_params=pltpu.CompilerParams(
            vmem_limit_bytes=56 * 2**20, collective_id=0, has_side_effects=True
        ),
    )(
        raw_samples, time, channel, shrink, grow, twiddle,
        filter_taps, units, dm_trials.reshape(1, DMS), tap,
    )
    return power[None]


def solution(mesh):
    in_specs = (P(("beam", "tm"), "freq"), P(None, "freq"), P(), P())
    out_specs = P(("beam", "tm"), "freq", None)
    return jax.shard_map(body, mesh=mesh, in_specs=in_specs, out_specs=out_specs, check_vma=False)
```

```python
import functools
import math

import jax
import jax.numpy as jnp
import numpy as np
from jax import lax
from jax.experimental import pallas as pl
from jax.experimental.pallas import tpu as pltpu
from jax.sharding import PartitionSpec as P

TAPS = 16
DFT_LEN = 2048
BINS = 256
SHARED = 512
DMS = 256
DM_STEPS = 1024
CHANNELS = 4096
RADIX = 16
INNER = CHANNELS // RADIX
CHUNK = 16
LANES = 128
SLAB = 256
KEPT = 160
TILE = 8


def band_basis():
    at = np.arange(SHARED)
    diag = ((SHARED - 1) / 2 - at) ** 2 * math.cos(2 * math.pi * BINS / DFT_LEN)
    off = at[1:] * (SHARED - at[1:]) / 2.0
    square = off * off
    low = np.full(KEPT, -float(SHARED * SHARED))
    high = np.full(KEPT, float(SHARED * SHARED))
    wanted = SHARED - np.arange(KEPT)
    for _ in range(70):
        middle = (low + high) / 2
        pivot = diag[0] - middle
        below = (pivot < 0).astype(np.int64)
        for row in range(1, SHARED):
            pivot = np.where(pivot == 0, 1e-30, pivot)
            pivot = diag[row] - middle - square[row - 1] / pivot
            below += pivot < 0
        high = np.where(below >= wanted, middle, high)
        low = np.where(below >= wanted, low, middle)
    value = (low + high) / 2
    down, up = np.zeros((SHARED, KEPT)), np.zeros((SHARED, KEPT))
    down[0], up[-1] = diag[0] - value, diag[-1] - value
    for row in range(1, SHARED):
        down[row] = diag[row] - value - square[row - 1] / down[row - 1]
        back = SHARED - 1 - row
        up[back] = diag[back] - value - square[back] / up[back + 1]
    twist = np.argmin(np.abs(down + up - (diag[:, None] - value)), 0)
    basis = np.zeros((SHARED, KEPT))
    basis[twist, np.arange(KEPT)] = 1.0
    for row in range(1, SHARED):
        basis[row] = np.where(row > twist, -off[row - 1] * basis[row - 1] / up[row], basis[row])
        back = SHARED - 1 - row
        step = -off[back] * basis[back + 1] / down[back]
        basis[back] = np.where(back < twist, step, basis[back])
    total = np.zeros(KEPT)
    for row in range(SHARED):
        total = total + basis[row] * basis[row]
    return (basis / np.sqrt(total)).T


def split(values, count):
    parts = []
    for _ in range(count):
        part = np.asarray(values).astype(jnp.bfloat16)
        parts.append(part)
        values = values - part.astype(np.float64)
    return parts


def bin_order(chips):
    groups = BINS // (2 * chips * TILE)
    bins = np.arange(BINS).reshape(groups, chips, 2, TILE)
    return bins.transpose(2, 1, 0, 3).reshape(-1)


def tables(chips):
    bins = bin_order(chips)[:, None]
    angle = 2 * np.pi * (bins * np.arange(DFT_LEN)[None, :] % DFT_LEN) / DFT_LEN
    time = np.concatenate([np.cos(angle), -np.sin(angle)], 0) / math.sqrt(DFT_LEN)
    basis = band_basis()
    shrink = np.concatenate(split(basis, 2), 0)
    grow = np.concatenate(split(np.dot(time[:, DFT_LEN - SHARED :], basis.T), 2), 1)
    angle = 2 * np.pi * (bins * np.arange(TAPS)[None, :]) / DFT_LEN
    tap = split(np.concatenate([np.cos(angle), -np.sin(angle)], 0), 3)
    tap = np.concatenate([tap[0], tap[1], tap[2], tap[0], tap[1], tap[0]], 1)
    ids = np.arange(INNER)
    start = (np.arange(chips) * (CHANNELS // chips))[:, None, None]
    angle = np.arange(RADIX)[:, None] * (ids[None, :] + start) % CHANNELS
    angle = 2 * np.pi * angle / CHANNELS
    twiddle = np.stack([np.cos(angle), -np.sin(angle)], 1) / math.sqrt(RADIX)
    spread = ids.reshape(CHANNELS // LANES, LANES // RADIX).T.reshape(-1)
    angle = 2 * np.pi * (ids[:, None] * spread[None, :] % INNER) / INNER
    cosine, sine = np.cos(angle), np.sin(angle)
    channel = np.block([[cosine, -sine], [sine, cosine]]) / math.sqrt(INNER)
    return (
        jnp.asarray(time[:, : DFT_LEN - SHARED], jnp.bfloat16),
        jnp.asarray(channel, jnp.bfloat16),
        jnp.asarray(shrink),
        jnp.asarray(grow),
        jnp.asarray(tap),
        jnp.asarray(twiddle, jnp.float32),
    )


def unit_circle(phase):
    x = phase.astype(jnp.float32) * (2.0 * math.pi / DFT_LEN)
    y = x * x
    sine, cosine = jnp.full_like(y, -1 / 39916800), jnp.full_like(y, 1 / 479001600)
    for value in (1 / 362880, -1 / 5040, 1 / 120, -1 / 6, 1.0):
        sine = sine * y + value
    for value in (-1 / 3628800, 1 / 40320, -1 / 720, 1 / 24, -0.5, 1.0):
        cosine = cosine * y + value
    return cosine, sine * x


def phasor(phase):
    quarter = (phase + 256) >> 9
    x = (phase - (quarter << 9)).astype(jnp.float32) * (2.0 * math.pi / DFT_LEN)
    y = x * x
    sine, cosine = jnp.full_like(y, 1 / 362880), jnp.full_like(y, 1 / 40320)
    for value in (-1 / 5040, 1 / 120, -1 / 6, 1.0):
        sine = sine * y + value
    for value in (-1 / 720, 1 / 24, -0.5, 1.0):
        cosine = cosine * y + value
    sine = sine * x
    odd = (quarter & 1) == 1
    swapped_cos = jnp.where(odd, -sine, cosine)
    swapped_sin = jnp.where(odd, cosine, sine)
    far = (quarter & 2) == 2
    return jnp.where(far, -swapped_cos, swapped_cos), jnp.where(far, -swapped_sin, swapped_sin)


def turn(real, imag, cosine, sine):
    return real * cosine - imag * sine, imag * cosine + real * sine


def fill_ramps(ramps, dms, first_bin, start, stop):
    groups = ramps.shape[0] // TILE

    @pl.loop(start, stop)
    def _(step):
        row = pl.multiple_of(step * CHUNK, CHUNK)
        units = lax.broadcasted_iota(jnp.int32, (CHUNK, DMS), 0) + (row + 1)
        delays = (units * dms[...]) >> 10
        step_cos, step_sin = unit_circle(delays)
        double = step_cos + step_cos
        group_cos, group_sin = phasor((delays * first_bin) & (DFT_LEN - 1))
        if groups > 1:
            jump_cos, jump_sin = phasor((delays * (BINS // groups)) & (DFT_LEN - 1))
        for group in range(groups):
            cosine, sine = group_cos, group_sin
            next_cos, next_sin = turn(cosine, sine, step_cos, step_sin)
            for at in range(TILE):
                ramps[group * TILE + at, pl.ds(row, CHUNK), :] = cosine.astype(jnp.bfloat16)
                ramps[group * TILE + at, pl.ds(SHARED + row, CHUNK), :] = sine.astype(jnp.bfloat16)
                if at + 2 < TILE:
                    last_cos, last_sin = cosine, sine
                    cosine, sine = next_cos, next_sin
                    next_cos, next_sin = double * cosine - last_cos, double * sine - last_sin
                else:
                    cosine, sine = next_cos, next_sin
            if group + 1 < groups:
                group_cos, group_sin = turn(group_cos, group_sin, jump_cos, jump_sin)


def dft(real, imag):
    count = len(real)
    if count == 1:
        return real, imag
    er, ei = dft(real[0::2], imag[0::2])
    odr, odi = dft(real[1::2], imag[1::2])
    half = count // 2
    outs = [None] * count
    for k in range(half):
        if k == 0:
            tr, ti = odr[k], odi[k]
        elif 4 * k == count:
            tr, ti = odi[k], -odr[k]
        else:
            c, s = math.cos(2 * math.pi * k / count), math.sin(2 * math.pi * k / count)
            tr, ti = odr[k] * c + odi[k] * s, odi[k] * c - odr[k] * s
        outs[k] = (er[k] + tr, ei[k] + ti)
        outs[k + half] = (er[k] - tr, ei[k] - ti)
    return [o[0] for o in outs], [o[1] for o in outs]


def channelize(pair, twiddle, first, half):
    cores, slabs, _, _, chips, size, wide = pair.shape
    bins = chips * size
    real, imag = [], []
    for core in range(cores):
        for slab in range(slabs):
            real.append(pair[core, slab, half, 0].astype(jnp.float32).reshape(bins, wide))
            imag.append(pair[core, slab, half, 1].astype(jnp.float32).reshape(bins, wide))
    join = max(1, INNER // wide)
    real = [jnp.concatenate(real[at : at + join], 1) for at in range(0, len(real), join)]
    imag = [jnp.concatenate(imag[at : at + join], 1) for at in range(0, len(imag), join)]
    fold = len(real)
    stride = RADIX // fold
    for r in range(stride):
        turned_real, turned_imag = [], []
        for f in range(fold):
            c, s = math.cos(2 * math.pi * r * f / RADIX), math.sin(2 * math.pi * r * f / RADIX)
            if r * f == 0:
                turned_real.append(real[f])
                turned_imag.append(imag[f])
            else:
                turned_real.append(real[f] * c + imag[f] * s)
                turned_imag.append(imag[f] * c - real[f] * s)
        outs_real, outs_imag = dft(turned_real, turned_imag)
        for at in range(fold):
            k2 = r + stride * at
            c, s = twiddle[0, k2 : k2 + 1, :], twiddle[1, k2 : k2 + 1, :]
            rows = slice(k2 * bins, k2 * bins + bins)
            value = outs_real[at] * c - outs_imag[at] * s
            first[rows, 0:INNER] = value.astype(jnp.bfloat16)
            value = outs_real[at] * s + outs_imag[at] * c
            first[rows, INNER:] = value.astype(jnp.bfloat16)


def fill_matches(matches, units):
    rows, lanes = units.shape
    ids = lax.broadcasted_iota(jnp.int32, (rows, SHARED), 1) + 1
    for k2 in range(RADIX):
        for at in range(lanes // RADIX):
            lane = at * RADIX + k2
            same = (units[:, lane : lane + 1] == ids).astype(jnp.float32)
            matches[k2, at * rows : (at + 1) * rows, :] = same.astype(jnp.bfloat16)


def group_units(spectra, matches, bins):
    whole = jnp.zeros((2 * bins, INNER), jnp.float32)
    pieces = []
    for k2 in range(RADIX):
        part = spectra[k2 * bins : (k2 + 1) * bins]
        part = jnp.concatenate([part[:, :INNER], part[:, INNER:]], 0)
        part = part.astype(jnp.bfloat16)
        whole += part.astype(jnp.float32)
        pieces.append(part)
    grouped = jnp.dot(
        jnp.concatenate(pieces, 1), matches[...].reshape(CHANNELS, SHARED),
        preferred_element_type=jnp.float32,
    )
    rest = jnp.sum(whole, 1, keepdims=True) - jnp.sum(grouped, 1, keepdims=True)
    return grouped, rest


def partner_order(members):
    return sorted(range(1, members), key=lambda o: -abs(o - members // 2))


def kernel(
    members, segments,
    raw, time_hbm, channel_hbm, shrink_hbm, grow_hbm, twiddle_hbm,
    filter_taps, units, dms, tap,
    out,
    own, time, channel, shrink, grow, twiddle, edges, later, tail, padded, spec, gain, extra,
    halves, pair, ramps, matches, first, kept_sums, kept_rest, sums_out, sums_in,
    power_out, power_in,
    local_sem, halo_send, halo_recv, pair_send, pair_recv, sum_send, sum_recv,
    pow_send, pow_recv,
):
    me = lax.axis_index("freq")
    seg = lax.axis_index("tm")
    chips = members // 2
    chip, core = me // 2, me % 2
    own_len, width = own.shape
    bins = BINS // members
    kept = DMS // members
    slabs, _, wide = later.shape
    head, rest = pl.ds(0, SHARED), pl.ds(SHARED, own_len - SHARED)
    loads = [
        pltpu.make_async_copy(raw.at[head], own.at[head], local_sem.at[0]),
        pltpu.make_async_copy(shrink_hbm, shrink, local_sem.at[1]),
        pltpu.make_async_copy(raw.at[rest], own.at[rest], local_sem.at[2]),
        pltpu.make_async_copy(time_hbm, time, local_sem.at[3]),
        pltpu.make_async_copy(grow_hbm, grow, local_sem.at[4]),
        pltpu.make_async_copy(channel_hbm, channel, local_sem.at[5]),
        pltpu.make_async_copy(twiddle_hbm.at[chip], twiddle, local_sem.at[6]),
    ]
    for load in loads[:2]:
        load.start()

    barrier = pltpu.get_barrier_semaphore()
    order = partner_order(members)
    near = [lax.rem(me + 2 * o, members) for o in range(1, chips)] + [me + 1 - 2 * core]
    for peer in near:
        pl.semaphore_signal(
            barrier, inc=1, device_id={"freq": peer}, device_id_type=pl.DeviceIdType.MESH
        )

    @pl.when(seg > 0)
    def _():
        pl.semaphore_signal(
            barrier, inc=1, device_id={"tm": seg - 1}, device_id_type=pl.DeviceIdType.MESH
        )

    @pl.when(seg < segments - 1)
    def _():
        pl.semaphore_signal(
            barrier, inc=1, device_id={"tm": seg + 1}, device_id_type=pl.DeviceIdType.MESH
        )

    @pl.when(seg == 0)
    def _():
        for load in loads[2:]:
            load.start()

    for load in loads[:2]:
        load.wait()

    @pl.when(seg > 0)
    def _():
        for load in loads[2:]:
            load.start()

    @pl.when(seg > 0)
    def _():
        both = jnp.dot(shrink[...], own[0:SHARED, :], preferred_element_type=jnp.float32)
        both = (both[:KEPT] + both[KEPT:]).astype(jnp.bfloat16)
        for slab in range(slabs):
            cols = slice(slab * wide, (slab + 1) * wide)
            edges[slab, 0:KEPT, :] = both[:, cols]
            edges[slab, KEPT:, :] = own[SHARED - TAPS : SHARED, cols]

    pl.semaphore_wait(
        barrier, len(near) + jnp.minimum(seg, 1) + jnp.minimum(segments - 1 - seg, 1)
    )

    def back_copy(slab):
        return pltpu.make_async_remote_copy(
            src_ref=edges.at[slab], dst_ref=later.at[slab],
            send_sem=halo_send.at[1 + slab], recv_sem=halo_recv.at[1 + slab],
            device_id={"tm": seg - 1}, device_id_type=pl.DeviceIdType.MESH,
        )

    def forward_copy():
        return pltpu.make_async_remote_copy(
            src_ref=raw.at[pl.ds(own_len - TAPS, TAPS)], dst_ref=tail,
            send_sem=halo_send.at[0], recv_sem=halo_recv.at[0],
            device_id={"tm": seg + 1}, device_id_type=pl.DeviceIdType.MESH,
        )

    @pl.when(seg > 0)
    def _():
        for slab in range(slabs):
            back_copy(slab).start()

    @pl.when(seg == 0)
    def _():
        tail[...] = jnp.zeros_like(tail)

    @pl.when(seg < segments - 1)
    def _():
        forward_copy().start()

    @pl.when(seg == segments - 1)
    def _():
        later[...] = jnp.zeros_like(later)

    taps = filter_taps[...]
    padded[0:TAPS, :] = taps.astype(jnp.float32)
    padded[TAPS:, :] = jnp.zeros((TAPS, width), jnp.float32)
    gain[...] = jnp.dot(
        tap[:, 0 : 3 * TAPS], jnp.concatenate([taps] * 3, 0),
        preferred_element_type=jnp.float32,
    )
    for load in loads[2:4]:
        load.wait()
    spec[...] = jnp.dot(time[...], own[...], preferred_element_type=jnp.float32)
    loads[4].wait()
    fill_matches(matches, units)
    first_bin = me * TILE
    fill_ramps(ramps, dms, first_bin, 0, 4)

    @pl.when(seg > 0)
    def _():
        forward_copy().wait_recv()

    _, _, parts, _, _, size, _ = pair.shape

    def pair_copy(slab, part):
        return pltpu.make_async_remote_copy(
            src_ref=halves.at[slab, part], dst_ref=pair.at[core, slab, part],
            send_sem=pair_send.at[slab, part], recv_sem=pair_recv.at[slab, part],
            device_id={"freq": me + 1 - 2 * core}, device_id_type=pl.DeviceIdType.MESH,
        )

    def block(half, part, at, cols):
        row = pl.multiple_of(half * (BINS // 2) + at * bins + part * size, size)
        up, low = pl.ds(row, size), pl.ds(BINS + row, size)
        sr, si, gr, gi = spec[up, cols], spec[low, cols], gain[up, cols], gain[low, cols]
        real = sr * gr - si * gi + extra[up, :]
        imag = sr * gi + si * gr + extra[low, :]
        return real.astype(jnp.bfloat16), imag.astype(jnp.bfloat16)

    for slab in range(slabs):
        cols = slice(slab * wide, (slab + 1) * wide)

        @pl.when(seg < segments - 1)
        def _():
            back_copy(slab).wait_recv()

        edge = tail[:, cols].astype(jnp.float32)
        edge = edge - later[slab, KEPT:, :].astype(jnp.float32)
        fringe = jnp.zeros_like(edge)
        for e in range(1, TAPS):
            fringe = fringe + padded[e : e + TAPS, cols] * edge[TAPS - e : TAPS - e + 1]
        fringe = fringe * (1.0 / math.sqrt(DFT_LEN))
        one = fringe.astype(jnp.bfloat16)
        left = fringe - one.astype(jnp.float32)
        two = left.astype(jnp.bfloat16)
        three = (left - two.astype(jnp.float32)).astype(jnp.bfloat16)
        extra[...] = jnp.dot(
            tap[...], jnp.concatenate([one, one, one, two, two, three], 0),
            preferred_element_type=jnp.float32,
        )
        spec[:, cols] += jnp.dot(
            grow[...], jnp.concatenate([later[slab, 0:KEPT, :]] * 2, 0),
            preferred_element_type=jnp.float32,
        )
        for part in range(parts):
            for at in range(chips):
                real, imag = block(1 - core, part, at, cols)
                halves[slab, part, 0, at], halves[slab, part, 1, at] = real, imag
            pair_copy(slab, part).start()
        for part in range(parts):
            for at in range(chips):
                real, imag = block(core, part, at, cols)
                pair[core, slab, part, 0, at], pair[core, slab, part, 1, at] = real, imag
        if slab + 1 < slabs:
            fill_ramps(ramps, dms, first_bin, 4, 8)
    fill_ramps(ramps, dms, first_bin, 8 if slabs > 1 else 4, 10)
    for load in loads[5:]:
        load.wait()

    def sum_copy(part, slot, target):
        sent = pl.ds(0, sums_in.shape[2] - (TAPS if part + 1 < parts else 0))
        return pltpu.make_async_remote_copy(
            src_ref=sums_out.at[part, target, sent], dst_ref=sums_in.at[part, slot, sent],
            send_sem=sum_send.at[part, target], recv_sem=sum_recv.at[part, slot],
            device_id={"freq": 2 * target + core}, device_id_type=pl.DeviceIdType.MESH,
        )

    ones = lax.broadcasted_iota(jnp.int32, (2 * size, LANES), 0)
    ones = (ones == lax.broadcasted_iota(jnp.int32, (2 * size, LANES), 1)).astype(jnp.float32)
    blocks = SHARED // LANES
    hops = partner_order(chips)[::-1]
    some = chips * size
    tall = 2 * size
    line_row = lax.broadcasted_iota(jnp.int32, (TAPS, LANES), 0)
    lines = [jnp.zeros((TAPS, LANES), jnp.float32)] * chips
    for part in range(parts):
        for slab in range(slabs):
            pair_copy(slab, part).wait_recv()
        channelize(pair, twiddle, first, part)
        spectra = jnp.dot(
            first[...], channel[...], preferred_element_type=jnp.float32
        )
        grouped, rest = group_units(spectra, matches, some)
        for at in range(chips):
            up = slice(at * size, (at + 1) * size)
            low = slice(some + at * size, some + (at + 1) * size)
            own_sums = jnp.concatenate([grouped[up], grouped[low]], 0)
            own_rest = jnp.concatenate([rest[up], rest[low]], 0)
            kept_sums[part, at] = own_sums
            kept_rest[part, at] = jnp.broadcast_to(own_rest, (2 * size, LANES))
            line = jnp.sum(own_rest * ones, 0, keepdims=True)
            high = line.astype(jnp.bfloat16).astype(jnp.float32)
            lines[at] = jnp.where(line_row == 2 * part, high, lines[at])
            lines[at] = jnp.where(line_row == 2 * part + 1, line - high, lines[at])
            pieces = [own_sums[:, lane * LANES : (lane + 1) * LANES] for lane in range(blocks)]
            pieces = jnp.concatenate(pieces, 0).astype(jnp.bfloat16)
            sums_out[part, at, 0 : blocks * tall, :] = pieces
            if part + 1 == parts:
                sums_out[part, at, blocks * tall :, :] = lines[at].astype(jnp.bfloat16)
        for o in hops:
            sum_copy(part, chip, lax.rem(chip + o, chips)).start()
    fill_ramps(ramps, dms, first_bin, 10, SHARED // CHUNK)
    totals = []
    tile_row = lax.broadcasted_iota(jnp.int32, (TILE, DMS), 0)
    for part in range(parts):
        grouped = kept_sums[part, chip]
        for o in hops:
            source = lax.rem(chip + o, chips)
            sum_copy(part, source, source).wait_recv()
            came = sums_in[part, source, 0 : blocks * tall, :].astype(jnp.float32)
            pieces = [came[at * tall : (at + 1) * tall] for at in range(blocks)]
            grouped += jnp.concatenate(pieces, 1)
        real, imag = grouped[:size], grouped[size:]
        upper = jnp.concatenate([real, -imag], 1)
        lower = jnp.concatenate([imag, real], 1)
        for group in range(size // TILE):
            tile = slice(group * TILE, (group + 1) * TILE)
            left = jnp.concatenate([upper[tile], lower[tile]], 0).astype(jnp.bfloat16)
            re = jnp.zeros((TILE, DMS), jnp.float32)
            im = jnp.zeros((TILE, DMS), jnp.float32)
            for at in range(TILE):
                total = jnp.dot(
                    left, ramps[part * size + group * TILE + at],
                    preferred_element_type=jnp.float32,
                )
                re = jnp.where(tile_row == at, total[:TILE], re)
                im = jnp.where(tile_row == at, total[TILE:], im)
            totals.append((re, im))
    powers = []
    for part in range(parts):
        rest = kept_rest[part, chip][:, 0:1]
        for o in hops:
            source = lax.rem(chip + o, chips)
            line = sums_in[parts - 1, source, blocks * tall :, :].astype(jnp.float32)
            line = line[2 * part : 2 * part + 1] + line[2 * part + 1 : 2 * part + 2]
            rest += jnp.sum(line * ones, 1, keepdims=True)
        for group in range(size // TILE):
            re, im = totals[part * (size // TILE) + group]
            re += rest[group * TILE : (group + 1) * TILE]
            im += rest[size + group * TILE : size + (group + 1) * TILE]
            powers.append((re * re + im * im) * (1.0 / CHANNELS))
    for target in range(members):
        cols = slice(target * kept, (target + 1) * kept)
        power_out[target] = jnp.concatenate([power[:, cols] for power in powers], 1)

    def power_copy(slot, target):
        return pltpu.make_async_remote_copy(
            src_ref=power_out.at[target], dst_ref=power_in.at[slot],
            send_sem=pow_send.at[target], recv_sem=pow_recv.at[slot],
            device_id={"freq": target}, device_id_type=pl.DeviceIdType.MESH,
        )

    for o in order:
        power_copy(me, lax.rem(me + o, members)).start()
    power_in[me] = power_out[me]
    for part in range(parts):
        for slab in range(slabs):
            pair_copy(slab, part).wait_send()
        for o in hops:
            target = lax.rem(chip + o, chips)
            sum_copy(part, target, target).wait_send()

    @pl.when(seg > 0)
    def _():
        for slab in range(slabs):
            back_copy(slab).wait_send()

    @pl.when(seg < segments - 1)
    def _():
        forward_copy().wait_send()
    for o in order:
        target = lax.rem(me + o, members)
        power_copy(target, target).wait_send()
    for o in order:
        target = lax.rem(me + o, members)
        power_copy(target, target).wait_recv()
    turned = jnp.concatenate([power_in[source] for source in range(members)], 0).T
    pieces = [turned[at * kept : (at + 1) * kept] for at in range(bins // TILE)]
    out[...] = jnp.concatenate(pieces, 1)


def body(raw_samples, filter_taps, dm_trials, channel_units):
    members = lax.axis_size("freq")
    own_len, width = raw_samples.shape
    bins, kept, wide = BINS // members, DMS // members, min(SLAB, width)
    slabs, rows = width // wide, KEPT + TAPS
    parts = 2 if bins % (2 * TAPS) == 0 else 1
    size = bins // parts
    swap = 2 * size * (SHARED // LANES) + TAPS
    chips = members // 2
    time, channel, shrink, grow, tap, twiddle = tables(chips)
    units = channel_units.reshape(CHANNELS // LANES, LANES)
    vmem = pl.BlockSpec(memory_space=pltpu.VMEM)
    anywhere = pl.BlockSpec(memory_space=pl.ANY)
    dma = pltpu.SemaphoreType.DMA
    power = pl.pallas_call(
        functools.partial(kernel, members, lax.axis_size("tm")),
        out_shape=pltpu.VMEM((kept, BINS), jnp.float32),
        in_specs=[anywhere] * 6 + [vmem] * 4,
        out_specs=vmem,
        scratch_shapes=[
            pltpu.VMEM((own_len, width), jnp.bfloat16),
            pltpu.VMEM(time.shape, jnp.bfloat16),
            pltpu.VMEM(channel.shape, jnp.bfloat16),
            pltpu.VMEM(shrink.shape, jnp.bfloat16),
            pltpu.VMEM(grow.shape, jnp.bfloat16),
            pltpu.VMEM(twiddle.shape[1:], jnp.float32),
            pltpu.VMEM((slabs, rows, wide), jnp.bfloat16),
            pltpu.VMEM((slabs, rows, wide), jnp.bfloat16),
            pltpu.VMEM((TAPS, width), jnp.bfloat16),
            pltpu.VMEM((2 * TAPS, width), jnp.float32),
            pltpu.VMEM((2 * BINS, width), jnp.float32),
            pltpu.VMEM((2 * BINS, width), jnp.float32),
            pltpu.VMEM((2 * BINS, wide), jnp.float32),
            pltpu.VMEM((slabs, parts, 2, chips, size, wide), jnp.bfloat16),
            pltpu.VMEM((2, slabs, parts, 2, chips, size, wide), jnp.bfloat16),
            pltpu.VMEM((bins, 2 * SHARED, DMS), jnp.bfloat16),
            pltpu.VMEM((RADIX, INNER, SHARED), jnp.bfloat16),
            pltpu.VMEM((RADIX * chips * size, 2 * INNER), jnp.bfloat16),
            pltpu.VMEM((parts, chips, 2 * size, SHARED), jnp.float32),
            pltpu.VMEM((parts, chips, 2 * size, LANES), jnp.float32),
            pltpu.VMEM((parts, chips, swap, LANES), jnp.bfloat16),
            pltpu.VMEM((parts, chips, swap, LANES), jnp.bfloat16),
            pltpu.VMEM((members, TILE, bins // TILE * kept), jnp.float32),
            pltpu.VMEM((members, TILE, bins // TILE * kept), jnp.float32),
            dma((7,)), dma((1 + slabs,)), dma((1 + slabs,)),
            dma((slabs, parts)), dma((slabs, parts)), dma((parts, chips)), dma((parts, chips)),
            dma((members,)), dma((members,)),
        ],
        compiler_params=pltpu.CompilerParams(
            vmem_limit_bytes=56 * 2**20, collective_id=0, has_side_effects=True
        ),
    )(
        raw_samples, time, channel, shrink, grow, twiddle,
        filter_taps, units, dm_trials.reshape(1, DMS), tap,
    )
    return power[None]


def solution(mesh):
    in_specs = (P(("beam", "tm"), "freq"), P(None, "freq"), P(), P())
    out_specs = P(("beam", "tm"), "freq", None)
    return jax.shard_map(body, mesh=mesh, in_specs=in_specs, out_specs=out_specs, check_vma=False)
```
